512 devices in a mesh: emb: 128 (over z, y, core), dp: 4 (over x).
Axes of the slice: x: 4, y: 8, z: 8, core: 2. Of those that a mesh axis runs over, the one named last changes fastest.
Arguments:
- table_rows: bfloat16 [262144, 128], P(('emb', 'dp')), may hold values from -0.359375 to 0.359375
- piece_ids: int32 [2555904, 4], P(('emb', 'dp')), may hold values from 0 to 511
- piece_counts: int32 [2555904], P(('emb', 'dp')), may hold values from 1 to 4
- piece_dest: int32 [2555904, 1], P(('emb', 'dp')), may hold values from 0 to 127, as said below
- piece_target: int32 [2555904], P(('emb', 'dp')), may hold values from 0 to 3327, as said below
- labels: int32 [65536], P(('emb', 'dp')), may hold values 0 or 1
- w_first: bfloat16 [3328, 1024], P('emb'), may hold values from -0.8984375 to 0.8984375
- w_second: bfloat16 [1024, 512], replicated, may hold values from -0.1875 to 0.1875
- w_third: bfloat16 [512, 256], replicated, may hold values from -0.25 to 0.25
- w_out: bfloat16 [256], replicated, may hold values from -0.375 to 0.375
Outputs:
- row_grad: float32 [262144, 128], P(('emb', 'dp'))
- grad_second: float32 [1024, 512], replicated
- grad_third: float32 [512, 256], replicated
- grad_out: float32 [256], replicated
The draws below stay inside these ranges and needn't reach their ends.
Inputs may be any that keep to these rules, and one draw needn't show every extreme that they name: `piece_dest`: at most 78 pieces of one device's block name the same destination, and every block has exactly 78 for one destination. `piece_target`: every bag of every sample block has at least one piece.
All inputs are finite; a program needn't handle non-finite values. No bound on the sum of `labels` on one device may be relied on, other than what follows from the above.
Results may differ from the reference program's by a relative error of at most 0.006.
Values may be sent and summed in bfloat16 or wider, within the bound.
A program may use at most 128 MiB of HBM per device.

```python
import jax
import jax.numpy as jnp
from jax import lax

FIELDS = 26
E = 128
H1 = 1024
H2 = 512
H3 = 256
K = 4
S_DEV = 128
P_DEV = 4992
TOUCH = 512
BATCH = 65536
P_ALL = 2555904
TOUCH_ALL = 262144
N_EMB = 128
N_DP = 4


def piece_layout(key):
    bags = S_DEV * FIELDS
    share = bags // N_EMB
    extra = bags // 2
    key_base, key_hot, key_extra, key_order = jax.random.split(key, 4)
    base_keys = jax.random.split(key_base, N_DP * N_EMB)
    perms = jax.vmap(lambda one: jax.random.permutation(one, bags))(base_keys)
    perms = perms.reshape(N_DP, N_EMB, N_EMB, share)
    base_target = jnp.transpose(perms, (2, 0, 1, 3)).reshape(N_EMB, N_DP, bags).astype(jnp.int32)
    base_dest = jnp.broadcast_to(jnp.repeat(jnp.arange(N_EMB, dtype=jnp.int32), share)[None, None, :], (N_EMB, N_DP, bags))
    hot = jax.random.randint(key_hot, (N_EMB, N_DP, 1), 0, N_EMB).astype(jnp.int32)
    slot = jnp.arange(extra, dtype=jnp.int32)[None, None, :]
    spread = (hot + 1 + jnp.maximum(slot - 2 * share, 0) % (N_EMB - 1)) % N_EMB
    extra_dest = jnp.where(slot < 2 * share, hot, spread).astype(jnp.int32)
    extra_target = jax.random.randint(key_extra, (N_EMB, N_DP, extra), 0, bags).astype(jnp.int32)
    dest = jnp.concatenate([base_dest, extra_dest], axis=-1)
    target = jnp.concatenate([base_target, extra_target], axis=-1)
    order_keys = jax.random.split(key_order, N_EMB * N_DP)
    order = jax.vmap(lambda one: jax.random.permutation(one, bags + extra))(order_keys).reshape(N_EMB, N_DP, bags + extra)
    dest = jnp.take_along_axis(dest, order, axis=-1)
    target = jnp.take_along_axis(target, order, axis=-1)
    return (dest.reshape(-1).astype(jnp.int32), target.reshape(-1).astype(jnp.int32))


def draw_piece_dest(key, part):
    dest, target = piece_layout(key)
    return dest.reshape(P_ALL, 1)


def draw_piece_target(key, part):
    dest, target = piece_layout(key)
    return target


def touch_ends(values, key, least, high):
    extent = values.shape
    place = [jax.random.randint(jax.random.fold_in(key, axis), (), 0, extent[axis]) for axis in range(len(extent))]
    values = values.at[tuple(place)].set(least)
    longest = extent.index(max(extent))
    place[longest] = (place[longest] + 1) % extent[longest]
    return values.at[tuple(place)].set(high)


def steps_of(own_key, extent, shards, least, top_value):
    def one(dim, parts):
        steps = jax.random.uniform(jax.random.fold_in(jax.random.fold_in(own_key, 6), dim), (parts,), jnp.float32, least / len(shards), top_value / len(shards))
        return jnp.repeat(jnp.exp(steps), extent[dim] // parts).reshape((-1,) + (1,) * (len(extent) - dim - 1))

    factor_of = one(*shards[0])
    for cut in shards[1:]:
        factor_of = factor_of * one(*cut)
    return factor_of


def centred(key, dims, deviation, bound, cuts=(), kind=jnp.bfloat16):
    values = jax.random.normal(key, dims, jnp.float32) * deviation
    if len(cuts) > 0:
        values = steps_of(key, dims, cuts, -0.22, 0.18) * values
    return jnp.clip(values, min=-bound, max=bound).astype(kind)


def setup_inputs(seed: int = 0) -> dict:
    seeds = jax.random.split(jax.random.key(seed), 11)
    return {
        "table_rows": centred(seeds[0], (TOUCH_ALL, E), 0.06, 0.359375, ((0, 512),)),
        "piece_ids": touch_ends(jax.random.randint(seeds[1], (P_ALL, K), 0, TOUCH), jax.random.fold_in(seeds[1], 1), 0, TOUCH - 1).astype(jnp.int32),
        "piece_counts": touch_ends(jax.random.randint(seeds[2], (P_ALL,), 1, K + 1), jax.random.fold_in(seeds[2], 1), 1, K).astype(jnp.int32),
        "piece_dest": draw_piece_dest(jax.random.fold_in(seeds[10], 71), 0),
        "piece_target": draw_piece_target(jax.random.fold_in(seeds[10], 71), 0),
        "labels": touch_ends((jax.random.randint(seeds[5], (BATCH,), 0, 2) < 1).astype(jnp.int32), jax.random.fold_in(seeds[5], 1), 0, 1),
        "w_first": centred(seeds[6], (FIELDS * E, H1), 0.15, 0.8984375, ((0, 128),)),
        "w_second": centred(seeds[7], (H1, H2), H1 ** -0.5, 0.1875),
        "w_third": centred(seeds[8], (H2, H3), H2 ** -0.5, 0.25),
        "w_out": centred(seeds[9], (H3,), H3 ** -0.5, 0.375),
    }


coef = 0.7978845608028654


def act_slope(values):
    inner = coef * (values + 0.044715 * values * values * values)
    tangent = jnp.tanh(inner)
    result = 0.5 * values * (1.0 + tangent)
    slope = 0.5 * (1.0 + tangent) + 0.5 * values * (1.0 - tangent * tangent) * coef * (1.0 + 3.0 * 0.044715 * values * values)
    return result, slope


def contract_last(left, right):
    return lax.dot_general(left, right, (((1,), (1,)), ((), ())), preferred_element_type=jnp.float32)


def contract_first(left, right):
    return lax.dot_general(left, right, (((0,), (0,)), ((), ())), preferred_element_type=jnp.float32)


def pool_block(block):
    rows, ids, counts = block
    live_ids = jnp.arange(ids.shape[1])[None, :] < counts[:, None]
    picked = rows[ids]
    picked = jnp.where(live_ids[:, :, None], picked, jnp.zeros_like(picked))
    return jnp.sum(picked, axis=1, dtype=jnp.float32).astype(jnp.bfloat16)


def row_block(block):
    ids, counts, grads = block
    live_ids = jnp.arange(ids.shape[1])[None, :] < counts[:, None]
    spread = jnp.where(live_ids[:, :, None], grads[:, None, :].astype(jnp.float32), jnp.float32(0.0))
    return jax.ops.segment_sum(spread.reshape(-1, E), ids.reshape(-1), num_segments=TOUCH)


def dense_step(features, truth, w_first, w_second, w_third, w_out):
    count = features.shape[0]
    first_act, first_slope = act_slope(jnp.dot(features, w_first, preferred_element_type=jnp.float32))
    first_act = first_act.astype(jnp.bfloat16)
    second_act, second_slope = act_slope(jnp.dot(first_act, w_second, preferred_element_type=jnp.float32))
    second_act = second_act.astype(jnp.bfloat16)
    third_act, third_slope = act_slope(jnp.dot(second_act, w_third, preferred_element_type=jnp.float32))
    third_act = third_act.astype(jnp.bfloat16)
    deep = jnp.dot(third_act, w_out, preferred_element_type=jnp.float32)
    vectors = features.reshape(count, FIELDS, E).astype(jnp.float32)
    total = jnp.sum(vectors, axis=1)
    pairs = 0.5 * jnp.sum(total * total - jnp.sum(vectors * vectors, axis=1), axis=1)
    logit_grad = jax.nn.sigmoid(deep + pairs) - truth
    grad_out = jnp.sum(logit_grad[:, None] * third_act.astype(jnp.float32), axis=0)
    third_grad = (logit_grad[:, None] * w_out.astype(jnp.float32)[None, :] * third_slope).astype(jnp.bfloat16)
    grad_third = contract_first(second_act, third_grad)
    second_grad = (contract_last(third_grad, w_third) * second_slope).astype(jnp.bfloat16)
    grad_second = contract_first(first_act, second_grad)
    first_grad = (contract_last(second_grad, w_second) * first_slope).astype(jnp.bfloat16)
    network = contract_last(first_grad, w_first).reshape(count, FIELDS, E)
    feature_grad = (network + logit_grad[:, None, None] * (total[:, None, :] - vectors)).astype(jnp.bfloat16)
    return feature_grad, grad_second, grad_third, grad_out


def reference(table_rows, piece_ids, piece_counts, piece_dest, piece_target, labels, w_first, w_second, w_third, w_out):
    rows_all = table_rows.reshape(N_EMB, N_DP, TOUCH, E)
    ids_all = piece_ids.reshape(N_EMB, N_DP, P_DEV, K)
    counts_all = piece_counts.reshape(N_EMB, N_DP, P_DEV)
    dest_all = piece_dest.reshape(N_EMB, N_DP, P_DEV)
    target_all = piece_target.reshape(N_EMB, N_DP, P_DEV)
    truth_all = labels.reshape(N_EMB, N_DP, S_DEV).astype(jnp.float32)
    grad_second = jnp.zeros((H1, H2), jnp.float32)
    grad_third = jnp.zeros((H2, H3), jnp.float32)
    grad_out = jnp.zeros((H3,), jnp.float32)
    row_parts = []
    for group in range(N_DP):
        ids = ids_all[:, group]
        counts = counts_all[:, group]
        pooled = lax.map(pool_block, (rows_all[:, group], ids, counts))
        segment = (dest_all[:, group] * (S_DEV * FIELDS) + target_all[:, group]).reshape(-1).astype(jnp.int32)
        bags = jax.ops.segment_sum(pooled.reshape(-1, E).astype(jnp.float32), segment, num_segments=N_EMB * S_DEV * FIELDS)
        features = bags.astype(jnp.bfloat16).reshape(N_EMB * S_DEV, FIELDS * E)
        truth = truth_all[:, group].reshape(-1)
        feature_grad, part_second, part_third, part_out = dense_step(features, truth, w_first, w_second, w_third, w_out)
        grad_second = grad_second + part_second
        grad_third = grad_third + part_third
        grad_out = grad_out + part_out
        piece_grad = feature_grad.reshape(-1, E)[segment].reshape(N_EMB, P_DEV, E)
        row_parts.append(lax.map(row_block, (ids, counts, piece_grad)))
    row_grad = jnp.stack(row_parts, axis=1).reshape(TOUCH_ALL, E)
    return row_grad, grad_second, grad_third, grad_out
```

```python
import jax
import jax.numpy as jnp
from jax import lax
from jax.experimental import pallas as pl
from jax.experimental.pallas import tpu as pltpu
from jax.sharding import PartitionSpec as P

FIELDS = 26
LANES = 128
CAP = 80
PIECE_CHUNK = 384
SHARD_ROWS = 26
PAD_ROWS = 32

BF = jnp.bfloat16
F32 = jnp.float32

coef = 0.7978845608028654


def act_slope(values):
    inner = coef * (values + 0.044715 * values * values * values)
    tangent = jnp.tanh(inner)
    result = 0.5 * values * (1.0 + tangent)
    slope = 0.5 * (1.0 + tangent) + 0.5 * values * (1.0 - tangent * tangent) * coef * (
        1.0 + 3.0 * 0.044715 * values * values
    )
    return (result, slope)


def contract(left, right, left_dim, right_dim):
    return lax.dot_general(
        left, right, (((left_dim,), (right_dim,)), ((), ())), preferred_element_type=F32
    )


def iota(shape, dim):
    return lax.broadcasted_iota(jnp.int32, shape, dim)


def one_hot(condition):
    return jnp.where(condition, 1.0, 0.0).astype(BF)


def slots_kernel(dest_ref, target_ref, count_ref, ids_ref, slots_ref):
    pieces = dest_ref.shape[1]
    shards = slots_ref.shape[1]
    chunk = PIECE_CHUNK
    before = one_hot(iota((chunk, chunk), 0) < iota((chunk, chunk), 1))
    carry = jnp.zeros((shards, 1), F32)
    total = None
    for step in range(pieces // chunk):
        part = slice(step * chunk, (step + 1) * chunk)
        is_dest = jnp.where(iota((shards, chunk), 0) == dest_ref[:, part], 1.0, 0.0)
        to_dest = is_dest.astype(BF)
        earlier = contract(to_dest, before, 1, 0) + carry
        rank = jnp.sum(is_dest * earlier, axis=0, keepdims=True)
        carry = carry + jnp.sum(is_dest, axis=1, keepdims=True)
        at_rank = one_hot(iota((LANES, chunk), 0).astype(F32) == rank)
        target = target_ref[:, part]
        sample = (target * 2521) // 65536
        field = target - sample * FIELDS
        count = count_ref[:, part]
        numbers = [field + 1, sample]
        for column in range(ids_ref.shape[0]):
            ids = ids_ref[column : column + 1, part]
            numbers.append(jnp.where(column < count, ids // LANES + 1, 0))
            numbers.append(ids % LANES)
        scaled = jnp.concatenate(
            [to_dest * number.astype(F32).astype(BF) for number in numbers], axis=0
        )
        placed = contract(scaled, at_rank, 1, 1)
        total = placed if total is None else total + placed
    for column in range(slots_ref.shape[0]):
        slots_ref[column] = total[column * shards : (column + 1) * shards]


def count_rows(high, low, height):
    slots = low[0].shape[1]
    lows = [one_hot(iota((LANES, slots), 0).astype(F32) == row) for row in low]
    tiles = []
    for tile in range(height):
        parts = [one * one_hot(row == tile + 1.0) for one, row in zip(lows, high)]
        tiles.append((parts[0] + parts[1]) + (parts[2] + parts[3]))
    return jnp.concatenate(tiles, axis=0)


def number_rows(numbers_ref, shards):
    def row(column):
        return jnp.concatenate([numbers_ref[column, pl.ds(one, 1)] for one in shards], axis=1)

    return [row(2 + 2 * k) for k in range(4)], [row(3 + 2 * k) for k in range(4)]


STEPS = 32


def quad(step):
    flip = step % 2
    place = (step // 2 * 7 + 2) % 16
    a, b = 1 + place // 4, place % 4
    last = 4 * ((place // 12) * ((4 - b) // 4))
    return flip, place, ((a, b), (8 - b, a), (8 + last - a, 8 - b), (b + last, 8 - a))


def shard_at(flip, move, sign):
    emb = lax.axis_index("emb")
    z = (emb // 16 + 8 + sign * move[0]) % 8
    y = ((emb // 2) % 8 + 8 + sign * move[1]) % 8
    return z * 16 + y * 2 + (emb + flip) % 2


def greet_all():
    emb = lax.axis_index("emb")
    barrier = pltpu.get_barrier_semaphore()

    def greet(step, carry):
        pl.semaphore_signal(
            barrier,
            inc=1,
            device_id={"emb": (emb + step) % LANES},
            device_id_type=pl.DeviceIdType.MESH,
        )
        return carry

    lax.fori_loop(1, LANES, greet, 0)
    return barrier


def send_block(step, which, flip, place, shard, send_ref, recv_ref, send_sem, recv_sem):
    emb = lax.axis_index("emb")
    source = send_ref.at[shard]
    target = recv_ref.at[emb, pl.ds(0, CAP)]

    def away():
        send_to({"emb": shard}, source, target, send_sem, recv_sem.at[step])

    if which != 2:
        away()
        return
    own = (place == 12) & (flip == 0)

    @pl.when(own)
    def _():
        pltpu.make_async_copy(source, target, recv_sem.at[step]).start()

    @pl.when(jnp.logical_not(own))
    def _():
        away()


def forward_kernel(
    numbers_ref, rows_ref, out_ref, owners_ref, send_ref, recv_ref, sums_ref, send_sem, recv_sem
):
    shards = recv_ref.shape[0]
    recv_ref[:, CAP:] = jnp.zeros((shards, LANES - CAP, LANES), BF)
    pl.semaphore_wait(greet_all(), LANES - 1)

    def send(step, carry):
        flip, place, moves = quad(step)
        for which, move in enumerate(moves):
            shard = shard_at(flip, move, 1)
            high, low = number_rows(numbers_ref, [shard])
            counts = count_rows(high, low, rows_ref.shape[0] // LANES)
            pooled = contract(counts, rows_ref[...], 0, 0)[:CAP]
            end = iota((8, LANES), 0)
            tail = jnp.where(end == 6, numbers_ref[0, pl.ds(shard, 1)], pooled[CAP - 8 :])
            tail = jnp.where(end == 7, numbers_ref[1, pl.ds(shard, 1)], tail)
            send_ref[shard] = jnp.concatenate([pooled[: CAP - 8], tail], axis=0).astype(BF)
            send_block(step, which, flip, place, shard, send_ref, recv_ref, send_sem, recv_sem)
        return carry

    lax.fori_loop(0, STEPS, send, 0)
    sums_ref[...] = jnp.zeros_like(sums_ref)

    def receive(step, carry):
        flip, _, moves = quad(step)
        wait_for(send_ref.at[pl.ds(0, 4)], recv_sem.at[step])
        arrived, fields, samples = [], [], []
        for move in moves:
            shard = shard_at(flip, move, -1)
            block = recv_ref[shard]
            tail = block[CAP - 16 : CAP].astype(F32)
            arrived.append(block)
            fields.append(tail[14:15])
            samples.append(tail[15:16])
            owners_ref[0, pl.ds(shard, 1)] = fields[-1]
            owners_ref[1, pl.ds(shard, 1)] = samples[-1]
        arrived = jnp.concatenate(arrived, axis=0)
        field = jnp.concatenate(fields, axis=1)
        sample = jnp.concatenate(samples, axis=1)
        in_sample = one_hot(iota((LANES, 4 * LANES), 0).astype(F32) == sample)
        for tile in range(FIELDS):
            member = in_sample * one_hot(field == tile + 1.0)
            sums_ref[tile] += jnp.dot(member, arrived, preferred_element_type=F32)
        return carry

    lax.fori_loop(0, STEPS, receive, 0)
    wait_for(send_ref.at[pl.ds(0, LANES - 1)], send_sem)
    for tile in range(FIELDS):
        out_ref[:, tile * LANES : (tile + 1) * LANES] = sums_ref[tile].astype(BF)


def window_tile(tile):
    start = tile * 4 * SHARD_ROWS
    return min(start // LANES, FIELDS - 2), start


def window_map(tile):
    first, start = window_tile(tile)
    feature = iota((2 * LANES, LANES), 0) + (first * LANES - start)
    place = iota((2 * LANES, LANES), 1)
    row = place % PAD_ROWS
    wanted = (place // PAD_ROWS) * SHARD_ROWS + row
    return jnp.where(row < SHARD_ROWS, one_hot(feature == wanted), jnp.zeros((), BF))


def dense_kernel(
    feature_ref, label_ref, first_ref, second_ref, third_ref, last_ref,
    grad_ref, packed_ref, padded_ref, network_ref,
):
    padded_tiles = first_ref.shape[0] // LANES
    for tile in range(padded_tiles):
        first, _ = window_tile(tile)
        window = feature_ref[:, first * LANES : (first + 2) * LANES]
        padded = jnp.dot(window, window_map(tile), preferred_element_type=F32)
        padded_ref[:, tile * LANES : (tile + 1) * LANES] = padded.astype(BF)
    first_pre = jnp.dot(padded_ref[...], first_ref[...], preferred_element_type=F32)
    first_act, first_slope = act_slope(first_pre)
    first_act = first_act.astype(BF)
    second_act, second_slope = act_slope(
        jnp.dot(first_act, second_ref[...], preferred_element_type=F32)
    )
    second_act = second_act.astype(BF)
    third_act, third_slope = act_slope(
        jnp.dot(second_act, third_ref[...], preferred_element_type=F32)
    )
    third_act = third_act.astype(BF).astype(F32)
    last = last_ref[...].astype(F32)
    deep = jnp.sum(third_act * last, axis=1, keepdims=True)
    total = jnp.zeros((feature_ref.shape[0], LANES), F32)
    squares = jnp.zeros((feature_ref.shape[0], LANES), F32)
    for tile in range(FIELDS):
        vector = feature_ref[:, tile * LANES : (tile + 1) * LANES].astype(F32)
        total = total + vector
        squares = squares + vector * vector
    pairs = 0.5 * jnp.sum(total * total - squares, axis=1, keepdims=True)
    logit_grad = jax.nn.sigmoid(deep + pairs) - label_ref[...].astype(F32)
    h1, h2 = second_ref.shape
    h3 = third_ref.shape[1]
    start = h1 * h2 // LANES
    end = start + h2 * h3 // LANES
    packed_ref[end:] = jnp.zeros_like(packed_ref[end:])
    grad_out = jnp.sum(logit_grad * third_act, axis=0, keepdims=True)
    for tile in range(h3 // LANES):
        packed_ref[end + 8 * tile : end + 8 * tile + 1] = grad_out[
            :, tile * LANES : (tile + 1) * LANES
        ]
    third_grad = (logit_grad * last * third_slope).astype(BF)
    grad_third = contract(second_act, third_grad, 0, 0)
    for tile in range(h3 // LANES):
        packed_ref[start + tile * h2 : start + (tile + 1) * h2] = grad_third[
            :, tile * LANES : (tile + 1) * LANES
        ]
    second_grad = (contract(third_grad, third_ref[...], 1, 1) * second_slope).astype(BF)
    for tile in range(h2 // LANES):
        packed_ref[tile * h1 : (tile + 1) * h1] = contract(
            first_act, second_grad[:, tile * LANES : (tile + 1) * LANES], 0, 0
        )
    first_grad = (contract(second_grad, second_ref[...], 1, 1) * first_slope).astype(BF)
    network_ref[...] = jnp.zeros_like(network_ref)
    for tile in range(padded_tiles):
        first, _ = window_tile(tile)
        part = contract(first_grad, first_ref[tile * LANES : (tile + 1) * LANES], 1, 1)
        upper = part.astype(BF)
        lower = (part - upper.astype(F32)).astype(BF)
        place = window_map(tile)
        moved = contract(upper, place, 1, 1) + contract(lower, place, 1, 1)
        network_ref[first] += moved[:, :LANES]
        network_ref[first + 1] += moved[:, LANES:]
    for tile in range(FIELDS):
        vector = feature_ref[:, tile * LANES : (tile + 1) * LANES].astype(F32)
        grad_ref[tile * LANES : (tile + 1) * LANES] = (
            network_ref[tile] + logit_grad * (total - vector)
        ).astype(BF)


def device(**axes):
    emb, dp = lax.axis_index("emb"), lax.axis_index("dp")
    z, y, core = emb // 16, (emb // 2) % 8, emb % 2
    z, y, core = axes.get("z", z), axes.get("y", y), axes.get("core", core)
    return {"emb": z * 16 + y * 2 + core, "dp": axes.get("x", dp)}


def send_to(partner, source, target, send_sem, recv_sem):
    pltpu.make_async_remote_copy(
        source,
        target,
        send_sem,
        recv_sem,
        device_id=partner,
        device_id_type=pl.DeviceIdType.MESH,
    ).start()


def wait_for(block, sem):
    pltpu.make_async_copy(block, block, sem).wait()


def reduce_steps(
    packed_ref, outs, full_ref, from_core, from_x, from_z, from_y, sum_core, sum_x, sum_z,
    send_sem, recv_sem,
):
    emb, x = lax.axis_index("emb"), lax.axis_index("dp")
    z, y, core = emb // 16, (emb // 2) % 8, emb % 2
    other = device(core=1 - core)

    def over_core():
        send_to(other, packed_ref.at[1 - core], from_core, send_sem.at[0], recv_sem.at[0])

    def over_x():
        wait_for(from_core, recv_sem.at[0])
        for part in range(4):
            sum_core[part] = packed_ref[core, part] + from_core[part]
        for step in range(1, 4):
            to = (x + step) % 4
            send_to(device(x=to), sum_core.at[to], from_x.at[x], send_sem.at[1], recv_sem.at[1])
        from_x[x] = sum_core[x]

    def over_z():
        wait_for(from_x.at[pl.ds(0, 3)], recv_sem.at[1])
        for part in range(8):
            sum_x[part] = (from_x[0, part] + from_x[1, part]) + (
                from_x[2, part] + from_x[3, part]
            )
        for step in range(1, 8):
            to = (z + step) % 8
            send_to(device(z=to), sum_x.at[to], from_z.at[z], send_sem.at[2], recv_sem.at[2])
        from_z[z] = sum_x[z]

    def over_y():
        wait_for(from_z.at[pl.ds(0, 7)], recv_sem.at[2])
        sum_z[...] = jnp.sum(from_z[...], axis=0)
        for step in range(1, 8):
            to = (y + step) % 8
            send_to(device(y=to), sum_z, from_y.at[y], send_sem.at[3], recv_sem.at[3])
        from_y[y] = sum_z[...]

    def gather_z():
        wait_for(from_y.at[pl.ds(0, 7)], recv_sem.at[3])
        full_ref[core, x, z] = jnp.sum(from_y[...], axis=0)
        mine = full_ref.at[core, x, z]
        for step in range(1, 8):
            send_to(device(z=(z + step) % 8), mine, mine, send_sem.at[4], recv_sem.at[4])

    def gather_x():
        wait_for(full_ref.at[core, x, pl.ds(0, 7)], recv_sem.at[4])
        mine = full_ref.at[core, x]
        for step in range(1, 4):
            send_to(device(x=(x + step) % 4), mine, mine, send_sem.at[5], recv_sem.at[5])

    def gather_core():
        wait_for(full_ref.at[core, pl.ds(0, 3)], recv_sem.at[5])
        mine = full_ref.at[core]
        send_to(other, mine, mine, send_sem.at[6], recv_sem.at[6])

    def finish():
        wait_for(full_ref.at[0], recv_sem.at[6])
        wait_for(from_core, send_sem.at[0])
        wait_for(from_x.at[pl.ds(0, 3)], send_sem.at[1])
        wait_for(from_z.at[pl.ds(0, 7)], send_sem.at[2])
        wait_for(from_y.at[pl.ds(0, 7)], send_sem.at[3])
        wait_for(full_ref.at[core, x, pl.ds(0, 7)], send_sem.at[4])
        wait_for(full_ref.at[core, pl.ds(0, 3)], send_sem.at[5])
        wait_for(full_ref.at[0], send_sem.at[6])
        for place, ref, column, row in grad_places(*outs):
            half, place = divmod(place, 4 * 8 * GRAD_ROWS)
            quarter, place = divmod(place, 8 * GRAD_ROWS)
            part, inside = divmod(place, GRAD_ROWS)
            ref[row : row + 8, column : column + LANES] = full_ref[
                half, quarter, part, inside : inside + 8
            ]

    return [over_core, over_x, over_z, over_y, gather_z, gather_x, gather_core, finish]


GRAD_ROWS = 88


def grad_places(second_ref, third_ref, out_ref):
    place = 0
    for ref in (second_ref, third_ref, out_ref):
        for column in range(0, ref.shape[1], LANES):
            for row in range(0, ref.shape[0], 8):
                yield place, ref, column, row
                place += 8


def backward_kernel(
    numbers_ref, owners_ref, grad_ref, packed_ref, out_ref, second_ref, third_ref, last_ref,
    send_ref, recv_ref, send_sem, recv_sem, *reduce_refs,
):
    x, shards = lax.axis_index("dp"), recv_ref.shape[0]
    recv_ref[:, CAP:] = jnp.zeros((shards, LANES - CAP, LANES), BF)
    out_ref[...] = jnp.zeros_like(out_ref)
    barrier = greet_all()
    for step in range(1, 4):
        pl.semaphore_signal(
            barrier,
            inc=1,
            device_id=device(x=(x + step) % 4),
            device_id_type=pl.DeviceIdType.MESH,
        )
    pl.semaphore_wait(barrier, LANES - 1 + 3)
    reduce = reduce_steps(packed_ref, (second_ref, third_ref, last_ref), *reduce_refs)

    def send(step, carry):
        flip, place, moves = quad(step)
        partners = [shard_at(flip, move, 1) for move in moves]
        members = []
        for shard in partners:
            square = (LANES, LANES)
            field = jnp.broadcast_to(owners_ref[0, pl.ds(shard, 1)], square).T[:CAP].astype(BF)
            sample = jnp.broadcast_to(owners_ref[1, pl.ds(shard, 1)], square).T[:CAP]
            in_sample = one_hot(iota((CAP, LANES), 1).astype(F32) == sample)
            none = jnp.zeros_like(in_sample)
            members.append(
                jnp.concatenate(
                    [
                        jnp.where(field == jnp.array(tile + 1.0, BF), in_sample, none)
                        for tile in range(FIELDS)
                    ],
                    axis=1,
                )
            )
        members = jnp.concatenate(members, axis=0)
        spread = jnp.dot(members, grad_ref[...], preferred_element_type=F32).astype(BF)
        for which, shard in enumerate(partners):
            send_ref[shard] = spread[which * CAP : (which + 1) * CAP]
            send_block(step, which, flip, place, shard, send_ref, recv_ref, send_sem, recv_sem)
        return carry

    def receive(step, carry):
        flip, _, moves = quad(step)
        wait_for(send_ref.at[pl.ds(0, 4)], recv_sem.at[step])
        partners = [shard_at(flip, move, -1) for move in moves]
        arrived = jnp.concatenate([recv_ref[shard] for shard in partners], axis=0)
        high, low = number_rows(numbers_ref, partners)
        counts = count_rows(high, low, out_ref.shape[0] // LANES)
        out_ref[...] += jnp.dot(counts, arrived, preferred_element_type=F32)
        return carry

    reduce[0]()
    lax.fori_loop(0, 8, send, 0)
    reduce[1]()
    lax.fori_loop(8, STEPS, send, 0)
    for part, reduce_step in enumerate(reduce[2:6]):
        reduce_step()
        lax.fori_loop(part * 8, part * 8 + 8, receive, 0)
    for reduce_step in reduce[6:]:
        reduce_step()
    wait_for(send_ref.at[pl.ds(0, LANES - 1)], send_sem)


PARAMS = pltpu.CompilerParams(vmem_limit_bytes=48 << 20)


def remote_params(collective_id):
    return pltpu.CompilerParams(
        vmem_limit_bytes=48 << 20, collective_id=collective_id, has_side_effects=True
    )


WHOLE = pl.BlockSpec(memory_space=pltpu.VMEM)


def cost(flops, bytes_accessed):
    return pl.CostEstimate(flops=flops, bytes_accessed=bytes_accessed, transcendentals=0)


def per_device(
    table_rows,
    piece_ids,
    piece_counts,
    piece_dest,
    piece_target,
    labels,
    w_first,
    w_second,
    w_third,
    w_out,
):
    shards = lax.axis_size("emb")
    pieces = piece_ids.shape[0]
    touched, width = table_rows.shape
    samples = labels.shape[0]
    h1, h2 = w_second.shape
    h3 = w_third.shape[1]
    slots = shards * CAP

    gathered = lax.all_gather(
        jnp.pad(w_first, ((0, PAD_ROWS - SHARD_ROWS), (0, 0))), "emb", axis=0, tiled=True
    )
    numbers = pl.pallas_call(
        slots_kernel,
        out_shape=jax.ShapeDtypeStruct((10, shards, LANES), F32),
        in_specs=[WHOLE] * 4,
        out_specs=WHOLE,
        compiler_params=PARAMS,
        cost_estimate=cost(2 * 1664 * pieces * LANES, 2_000_000),
    )(
        piece_dest.reshape(1, pieces),
        piece_target.reshape(1, pieces),
        piece_counts.reshape(1, pieces),
        piece_ids.T,
    )
    exchange = [
        pltpu.VMEM((shards, CAP, width), BF),
        pltpu.VMEM((shards, LANES, width), BF),
    ]
    features, owners = pl.pallas_call(
        forward_kernel,
        out_shape=(
            jax.ShapeDtypeStruct((samples, FIELDS * width), BF),
            jax.ShapeDtypeStruct((2, shards, LANES), F32),
        ),
        in_specs=[WHOLE] * 2,
        out_specs=(WHOLE,) * 2,
        scratch_shapes=exchange
        + [
            pltpu.VMEM((FIELDS, samples, width), F32),
            pltpu.SemaphoreType.DMA,
            pltpu.SemaphoreType.DMA((STEPS,)),
        ],
        compiler_params=remote_params(0),
        cost_estimate=cost(2 * slots * FIELDS * samples * width, 200_000_000),
    )(numbers, table_rows)
    feature_grad, packed = pl.pallas_call(
        dense_kernel,
        out_shape=(
            jax.ShapeDtypeStruct((FIELDS * samples, width), BF),
            jax.ShapeDtypeStruct((64 * GRAD_ROWS, LANES), F32),
        ),
        in_specs=[WHOLE] * 6,
        out_specs=(WHOLE,) * 2,
        scratch_shapes=[
            pltpu.VMEM((samples, shards * PAD_ROWS), BF),
            pltpu.VMEM((FIELDS, samples, width), F32),
        ],
        compiler_params=PARAMS,
        cost_estimate=cost(6 * samples * shards * PAD_ROWS * h1, 16_000_000),
    )(features, labels.reshape(samples, 1), gathered, w_second, w_third, w_out.reshape(1, h3))
    part = (GRAD_ROWS, LANES)
    row_grad, grad_second, grad_third, grad_out = pl.pallas_call(
        backward_kernel,
        out_shape=(
            jax.ShapeDtypeStruct((touched, width), F32),
            jax.ShapeDtypeStruct((h1, h2), F32),
            jax.ShapeDtypeStruct((h2, h3), F32),
            jax.ShapeDtypeStruct((8, h3), F32),
        ),
        in_specs=[WHOLE] * 4,
        out_specs=(WHOLE,) * 4,
        scratch_shapes=exchange
        + [
            pltpu.SemaphoreType.DMA,
            pltpu.SemaphoreType.DMA((STEPS,)),
            pltpu.VMEM((2, 4, 8) + part, F32),
            pltpu.VMEM((4, 8) + part, F32),
            pltpu.VMEM((4, 8) + part, F32),
            pltpu.VMEM((8,) + part, F32),
            pltpu.VMEM((8,) + part, F32),
            pltpu.VMEM((4, 8) + part, F32),
            pltpu.VMEM((8,) + part, F32),
            pltpu.VMEM(part, F32),
            pltpu.SemaphoreType.DMA((7,)),
            pltpu.SemaphoreType.DMA((7,)),
        ],
        compiler_params=remote_params(1),
        cost_estimate=cost(2 * slots * FIELDS * samples * width, 200_000_000),
    )(numbers, owners, feature_grad, packed.reshape((2, 4, 8) + part))
    return (row_grad, grad_second, grad_third, grad_out[0])


def solution(mesh):
    in_specs = (
        P(("emb", "dp"), None),
        P(("emb", "dp"), None),
        P(("emb", "dp")),
        P(("emb", "dp"), None),
        P(("emb", "dp")),
        P(("emb", "dp")),
        P("emb", None),
        P(),
        P(),
        P(),
    )
    out_specs = (P(("emb", "dp"), None), P(), P(), P())
    return jax.shard_map(
        per_device, mesh=mesh, in_specs=in_specs, out_specs=out_specs, check_vma=False
    )
```

```python
import jax
import jax.numpy as jnp
from jax import lax
from jax.experimental import pallas as pl
from jax.experimental.pallas import tpu as pltpu
from jax.sharding import PartitionSpec as P

FIELDS = 26
LANES = 128
CAP = 80
PIECE_CHUNK = 384
SHARD_ROWS = 26
PAD_ROWS = 32

BF = jnp.bfloat16
F32 = jnp.float32

coef = 0.7978845608028654


def act_slope(values):
    inner = coef * (values + 0.044715 * values * values * values)
    tangent = jnp.tanh(inner)
    result = 0.5 * values * (1.0 + tangent)
    slope = 0.5 * (1.0 + tangent) + 0.5 * values * (1.0 - tangent * tangent) * coef * (
        1.0 + 3.0 * 0.044715 * values * values
    )
    return (result, slope)


def contract(left, right, left_dim, right_dim):
    return lax.dot_general(
        left, right, (((left_dim,), (right_dim,)), ((), ())), preferred_element_type=F32
    )


def iota(shape, dim):
    return lax.broadcasted_iota(jnp.int32, shape, dim)


def one_hot(condition):
    return jnp.where(condition, 1.0, 0.0).astype(BF)


def slots_kernel(dest_ref, target_ref, count_ref, ids_ref, slots_ref):
    pieces = dest_ref.shape[1]
    shards = slots_ref.shape[1]
    chunk = PIECE_CHUNK
    before = one_hot(iota((chunk, chunk), 0) < iota((chunk, chunk), 1))
    carry = jnp.zeros((shards, 1), F32)
    total = None
    for step in range(pieces // chunk):
        part = slice(step * chunk, (step + 1) * chunk)
        is_dest = jnp.where(iota((shards, chunk), 0) == dest_ref[:, part], 1.0, 0.0)
        to_dest = is_dest.astype(BF)
        earlier = contract(to_dest, before, 1, 0) + carry
        rank = jnp.sum(is_dest * earlier, axis=0, keepdims=True)
        carry = carry + jnp.sum(is_dest, axis=1, keepdims=True)
        at_rank = one_hot(iota((LANES, chunk), 0).astype(F32) == rank)
        target = target_ref[:, part]
        sample = (target * 2521) // 65536
        field = target - sample * FIELDS
        count = count_ref[:, part]
        numbers = [field + 1, sample]
        for column in range(ids_ref.shape[0]):
            ids = ids_ref[column : column + 1, part]
            numbers.append(jnp.where(column < count, ids // LANES + 1, 0))
            numbers.append(ids % LANES)
        scaled = jnp.concatenate(
            [to_dest * number.astype(F32).astype(BF) for number in numbers], axis=0
        )
        placed = contract(scaled, at_rank, 1, 1)
        total = placed if total is None else total + placed
    for column in range(slots_ref.shape[0]):
        slots_ref[column] = total[column * shards : (column + 1) * shards]


def count_rows(high, low, height):
    slots = low[0].shape[1]
    lows = [one_hot(iota((LANES, slots), 0).astype(F32) == row) for row in low]
    tiles = []
    for tile in range(height):
        parts = [one * one_hot(row == tile + 1.0) for one, row in zip(lows, high)]
        tiles.append((parts[0] + parts[1]) + (parts[2] + parts[3]))
    return jnp.concatenate(tiles, axis=0)


def number_rows(numbers_ref, shards):
    def row(column):
        return jnp.concatenate([numbers_ref[column, pl.ds(one, 1)] for one in shards], axis=1)

    return [row(2 + 2 * k) for k in range(4)], [row(3 + 2 * k) for k in range(4)]


STEPS = 32
LAG = 10


def quad(step):
    flip = step % 2
    place = (step // 2 * 7 + 2) % 16
    a, b = 1 + place // 4, place % 4
    last = 4 * ((place // 12) * ((4 - b) // 4))
    return flip, place, ((a, b), (8 - b, a), (8 + last - a, 8 - b), (b + last, 8 - a))


def shard_at(flip, move, sign):
    emb = lax.axis_index("emb")
    z = (emb // 16 + 8 + sign * move[0]) % 8
    y = ((emb // 2) % 8 + 8 + sign * move[1]) % 8
    return z * 16 + y * 2 + (emb + flip) % 2


def greet_all():
    emb = lax.axis_index("emb")
    barrier = pltpu.get_barrier_semaphore()

    def greet(step, carry):
        pl.semaphore_signal(
            barrier,
            inc=1,
            device_id={"emb": (emb + step) % LANES},
            device_id_type=pl.DeviceIdType.MESH,
        )
        return carry

    lax.fori_loop(1, LANES, greet, 0)
    return barrier


def send_block(step, which, flip, place, shard, send_ref, recv_ref, send_sem, recv_sem):
    emb = lax.axis_index("emb")
    source = send_ref.at[shard]
    target = recv_ref.at[emb, pl.ds(0, CAP)]

    def away():
        send_to({"emb": shard}, source, target, send_sem, recv_sem.at[step])

    if which != 2:
        away()
        return
    own = (place == 12) & (flip == 0)

    @pl.when(own)
    def _():
        pltpu.make_async_copy(source, target, recv_sem.at[step]).start()

    @pl.when(jnp.logical_not(own))
    def _():
        away()


def gather_steps(shard_ref, full_ref, send_sem, recv_sem):
    emb, x = lax.axis_index("emb"), lax.axis_index("dp")
    z, y, core = emb // 16, (emb // 2) % 8, emb % 2
    other = device(core=1 - core)
    first, second = 2 * x, 2 * x + 1

    def start():
        for block in (first, second):
            full_ref[block, z, y, core] = shard_ref[block]
        for step in range(1, 8):
            mine = full_ref.at[first, z, y, core]
            send_to(device(z=(z + step) % 8), mine, mine, send_sem.at[0], recv_sem.at[0])
            mine = full_ref.at[second, z, y, core]
            send_to(device(y=(y + step) % 8), mine, mine, send_sem.at[1], recv_sem.at[1])

    def lines():
        wait_for(full_ref.at[first, pl.ds(0, 7), y, core], recv_sem.at[0])
        wait_for(full_ref.at[second, z, pl.ds(0, 7), core], recv_sem.at[1])
        for step in range(1, 8):
            mine = full_ref.at[first, :, y, core]
            send_to(device(y=(y + step) % 8), mine, mine, send_sem.at[2], recv_sem.at[2])
            mine = full_ref.at[second, z, :, core]
            send_to(device(z=(z + step) % 8), mine, mine, send_sem.at[3], recv_sem.at[3])

    def over_x():
        wait_for(full_ref.at[first, :, pl.ds(0, 7), core], recv_sem.at[2])
        wait_for(full_ref.at[second, pl.ds(0, 7), :, core], recv_sem.at[3])
        mine = full_ref.at[pl.ds(first, 2), :, :, core]
        for step in range(1, 4):
            send_to(device(x=(x + step) % 4), mine, mine, send_sem.at[4], recv_sem.at[3 + step])
        send_to(other, mine, mine, send_sem.at[5], recv_sem.at[7])

    def over_core(step):
        def forward():
            mine = full_ref.at[pl.ds(2 * ((x + 4 - step) % 4), 2), :, :, core]
            wait_for(mine, recv_sem.at[3 + step])
            send_to(other, mine, mine, send_sem.at[5], recv_sem.at[7])

        return forward

    def finish():
        wait_for(full_ref.at[:, :, :, core], recv_sem.at[7])
        wait_for(full_ref.at[first, pl.ds(0, 7), y, core], send_sem.at[0])
        wait_for(full_ref.at[second, z, pl.ds(0, 7), core], send_sem.at[1])
        wait_for(full_ref.at[first, :, pl.ds(0, 7), core], send_sem.at[2])
        wait_for(full_ref.at[second, pl.ds(0, 7), :, core], send_sem.at[3])
        wait_for(full_ref.at[pl.ds(0, 6), :, :, core], send_sem.at[4])
        wait_for(full_ref.at[:, :, :, core], send_sem.at[5])

    return [start, lines, over_x, over_core(1), over_core(3), over_core(2), finish]


def greet_x(barrier):
    x = lax.axis_index("dp")
    for step in range(1, 4):
        pl.semaphore_signal(
            barrier,
            inc=1,
            device_id=device(x=(x + step) % 4),
            device_id_type=pl.DeviceIdType.MESH,
        )


def paced_exchange(send, receive, others):
    def one(step, carry):
        for at, other in others:
            pl.when(step == at)(other)

        @pl.when(step < STEPS)
        def _():
            send(step)

        @pl.when(step >= LAG)
        def _():
            receive(step - LAG)

        return carry

    lax.fori_loop(0, STEPS + LAG, one, 0)


def forward_kernel(
    numbers_ref, rows_ref, shard_ref, out_ref, owners_ref, full_ref,
    send_ref, recv_ref, sums_ref, send_sem, recv_sem, gather_send, gather_recv,
):
    shards = recv_ref.shape[0]
    gather = gather_steps(shard_ref, full_ref, gather_send, gather_recv)
    barrier = greet_all()
    greet_x(barrier)
    recv_ref[:, CAP:] = jnp.zeros((shards, LANES - CAP, LANES), BF)
    sums_ref[...] = jnp.zeros_like(sums_ref)
    pl.semaphore_wait(barrier, LANES - 1 + 3)
    gather[0]()

    def send(step):
        flip, place, moves = quad(step)
        for which, move in enumerate(moves):
            shard = shard_at(flip, move, 1)
            high, low = number_rows(numbers_ref, [shard])
            counts = count_rows(high, low, rows_ref.shape[0] // LANES)
            pooled = contract(counts, rows_ref[...], 0, 0)[:CAP]
            end = iota((8, LANES), 0)
            tail = jnp.where(end == 6, numbers_ref[0, pl.ds(shard, 1)], pooled[CAP - 8 :])
            tail = jnp.where(end == 7, numbers_ref[1, pl.ds(shard, 1)], tail)
            send_ref[shard] = jnp.concatenate([pooled[: CAP - 8], tail], axis=0).astype(BF)
            send_block(step, which, flip, place, shard, send_ref, recv_ref, send_sem, recv_sem)

    def receive(step):
        flip, _, moves = quad(step)
        wait_for(send_ref.at[pl.ds(0, 4)], recv_sem.at[step])
        arrived, fields, samples = [], [], []
        for move in moves:
            shard = shard_at(flip, move, -1)
            block = recv_ref[shard]
            tail = block[CAP - 16 : CAP].astype(F32)
            arrived.append(block)
            fields.append(tail[14:15])
            samples.append(tail[15:16])
            owners_ref[0, pl.ds(shard, 1)] = fields[-1]
            owners_ref[1, pl.ds(shard, 1)] = samples[-1]
        arrived = jnp.concatenate(arrived, axis=0)
        field = jnp.concatenate(fields, axis=1)
        sample = jnp.concatenate(samples, axis=1)
        in_sample = one_hot(iota((LANES, 4 * LANES), 0).astype(F32) == sample)
        for tile in range(FIELDS):
            member = in_sample * one_hot(field == tile + 1.0)
            sums_ref[tile] += jnp.dot(member, arrived, preferred_element_type=F32)

    paced_exchange(
        send,
        receive,
        [(1, gather[1]), (8, gather[2]), (32, gather[3]), (34, gather[4]), (38, gather[5])],
    )
    wait_for(send_ref.at[pl.ds(0, LANES - 1)], send_sem)
    for tile in range(FIELDS):
        out_ref[:, tile * LANES : (tile + 1) * LANES] = sums_ref[tile].astype(BF)
    gather[6]()


def window_tile(tile):
    start = tile * 4 * SHARD_ROWS
    return min(start // LANES, FIELDS - 2), start


def window_map(tile):
    first, start = window_tile(tile)
    feature = iota((2 * LANES, LANES), 0) + (first * LANES - start)
    place = iota((2 * LANES, LANES), 1)
    row = place % PAD_ROWS
    wanted = (place // PAD_ROWS) * SHARD_ROWS + row
    return jnp.where(row < SHARD_ROWS, one_hot(feature == wanted), jnp.zeros((), BF))


def dense_kernel(
    feature_ref, label_ref, first_ref, second_ref, third_ref, last_ref,
    grad_ref, packed_ref, padded_ref, network_ref,
):
    blocks, padded_rows, _ = first_ref.shape
    padded_tiles = padded_rows // LANES
    for tile in range(padded_tiles):
        first, _ = window_tile(tile)
        window = feature_ref[:, first * LANES : (first + 2) * LANES]
        padded = jnp.dot(window, window_map(tile), preferred_element_type=F32)
        padded_ref[:, tile * LANES : (tile + 1) * LANES] = padded.astype(BF)
    first_pre = jnp.concatenate(
        [
            jnp.dot(padded_ref[...], first_ref[block], preferred_element_type=F32)
            for block in range(blocks)
        ],
        axis=1,
    )
    first_act, first_slope = act_slope(first_pre)
    first_act = first_act.astype(BF)
    second_act, second_slope = act_slope(
        jnp.dot(first_act, second_ref[...], preferred_element_type=F32)
    )
    second_act = second_act.astype(BF)
    third_act, third_slope = act_slope(
        jnp.dot(second_act, third_ref[...], preferred_element_type=F32)
    )
    third_act = third_act.astype(BF).astype(F32)
    last = last_ref[...].astype(F32)
    deep = jnp.sum(third_act * last, axis=1, keepdims=True)
    total = jnp.zeros((feature_ref.shape[0], LANES), F32)
    squares = jnp.zeros((feature_ref.shape[0], LANES), F32)
    for tile in range(FIELDS):
        vector = feature_ref[:, tile * LANES : (tile + 1) * LANES].astype(F32)
        total = total + vector
        squares = squares + vector * vector
    pairs = 0.5 * jnp.sum(total * total - squares, axis=1, keepdims=True)
    logit_grad = jax.nn.sigmoid(deep + pairs) - label_ref[...].astype(F32)
    h1, h2 = second_ref.shape
    h3 = third_ref.shape[1]
    start = h1 * h2 // LANES
    end = start + h2 * h3 // LANES
    packed_ref[end:] = jnp.zeros_like(packed_ref[end:])
    grad_out = jnp.sum(logit_grad * third_act, axis=0, keepdims=True)
    for tile in range(h3 // LANES):
        packed_ref[end + 16 * tile : end + 16 * tile + 1] = grad_out[
            :, tile * LANES : (tile + 1) * LANES
        ]
    third_grad = (logit_grad * last * third_slope).astype(BF)
    grad_third = contract(second_act, third_grad, 0, 0)
    for tile in range(h3 // LANES):
        packed_ref[start + tile * h2 : start + (tile + 1) * h2] = grad_third[
            :, tile * LANES : (tile + 1) * LANES
        ]
    second_grad = (contract(third_grad, third_ref[...], 1, 1) * second_slope).astype(BF)
    for tile in range(h2 // LANES):
        packed_ref[tile * h1 : (tile + 1) * h1] = contract(
            first_act, second_grad[:, tile * LANES : (tile + 1) * LANES], 0, 0
        )
    first_grad = (contract(second_grad, second_ref[...], 1, 1) * first_slope).astype(BF)
    network_ref[...] = jnp.zeros_like(network_ref)
    for tile in range(padded_tiles):
        first, _ = window_tile(tile)
        rows = slice(tile * LANES, (tile + 1) * LANES)
        weights = jnp.concatenate([first_ref[block, rows] for block in range(blocks)], axis=1)
        part = contract(first_grad, weights, 1, 1)
        upper = part.astype(BF)
        lower = (part - upper.astype(F32)).astype(BF)
        place = window_map(tile)
        moved = contract(upper, place, 1, 1) + contract(lower, place, 1, 1)
        network_ref[first] += moved[:, :LANES]
        network_ref[first + 1] += moved[:, LANES:]
    for tile in range(FIELDS):
        vector = feature_ref[:, tile * LANES : (tile + 1) * LANES].astype(F32)
        grad_ref[tile * LANES : (tile + 1) * LANES] = (
            network_ref[tile] + logit_grad * (total - vector)
        ).astype(BF)


def device(**axes):
    emb, dp = lax.axis_index("emb"), lax.axis_index("dp")
    z, y, core = emb // 16, (emb // 2) % 8, emb % 2
    z, y, core = axes.get("z", z), axes.get("y", y), axes.get("core", core)
    return {"emb": z * 16 + y * 2 + core, "dp": axes.get("x", dp)}


def send_to(partner, source, target, send_sem, recv_sem):
    pltpu.make_async_remote_copy(
        source,
        target,
        send_sem,
        recv_sem,
        device_id=partner,
        device_id_type=pl.DeviceIdType.MESH,
    ).start()


def wait_for(block, sem):
    pltpu.make_async_copy(block, block, sem).wait()


def reduce_steps(
    packed_ref, outs, full_ref, from_core, from_x, from_z, from_y, sum_core, sum_x, sum_z,
    send_sem, recv_sem,
):
    emb, x = lax.axis_index("emb"), lax.axis_index("dp")
    z, y, core = emb // 16, (emb // 2) % 8, emb % 2
    other = device(core=1 - core)

    def over_core():
        send_to(other, packed_ref.at[1 - core], from_core, send_sem.at[0], recv_sem.at[0])

    def over_x():
        wait_for(from_core, recv_sem.at[0])
        for part in range(4):
            sum_core[part] = packed_ref[core, part] + from_core[part]
        for step in range(1, 4):
            to = (x + step) % 4
            send_to(device(x=to), sum_core.at[to], from_x.at[x], send_sem.at[1], recv_sem.at[1])
        from_x[x] = sum_core[x]

    def over_z():
        wait_for(from_x.at[pl.ds(0, 3)], recv_sem.at[1])
        for part in range(8):
            total = (from_x[0, part] + from_x[1, part]) + (from_x[2, part] + from_x[3, part])
            sum_x[part] = total.astype(BF)
        for step in range(1, 8):
            to = (z + step) % 8
            send_to(device(z=to), sum_x.at[to], from_z.at[z], send_sem.at[2], recv_sem.at[2])
        from_z[z] = sum_x[z]

    def over_y():
        wait_for(from_z.at[pl.ds(0, 7)], recv_sem.at[2])
        sum_z[...] = jnp.sum(from_z[...].astype(F32), axis=0).astype(BF)
        for step in range(1, 8):
            to = (y + step) % 8
            send_to(device(y=to), sum_z, from_y.at[y], send_sem.at[3], recv_sem.at[3])
        from_y[y] = sum_z[...]

    def gather_z():
        wait_for(from_y.at[pl.ds(0, 7)], recv_sem.at[3])
        full_ref[core, x, z] = jnp.sum(from_y[...].astype(F32), axis=0).astype(BF)
        mine = full_ref.at[core, x, z]
        for step in range(1, 8):
            send_to(device(z=(z + step) % 8), mine, mine, send_sem.at[4], recv_sem.at[4])

    def gather_x():
        wait_for(full_ref.at[core, x, pl.ds(0, 7)], recv_sem.at[4])
        mine = full_ref.at[core, x]
        for step in range(1, 4):
            send_to(device(x=(x + step) % 4), mine, mine, send_sem.at[5], recv_sem.at[5])

    def gather_core():
        wait_for(full_ref.at[core, pl.ds(0, 3)], recv_sem.at[5])
        mine = full_ref.at[core]
        send_to(other, mine, mine, send_sem.at[6], recv_sem.at[6])

    def finish():
        wait_for(full_ref.at[0], recv_sem.at[6])
        wait_for(from_core, send_sem.at[0])
        wait_for(from_x.at[pl.ds(0, 3)], send_sem.at[1])
        wait_for(from_z.at[pl.ds(0, 7)], send_sem.at[2])
        wait_for(from_y.at[pl.ds(0, 7)], send_sem.at[3])
        wait_for(full_ref.at[core, x, pl.ds(0, 7)], send_sem.at[4])
        wait_for(full_ref.at[core, pl.ds(0, 3)], send_sem.at[5])
        wait_for(full_ref.at[0], send_sem.at[6])
        for place, ref, column, row in grad_places(*outs):
            half, place = divmod(place, 4 * 8 * GRAD_ROWS)
            quarter, place = divmod(place, 8 * GRAD_ROWS)
            part, inside = divmod(place, GRAD_ROWS)
            block = full_ref[half, quarter, part, inside : inside + 16]
            ref[row : row + 16, column : column + LANES] = block.astype(F32)

    return [over_core, over_x, over_z, over_y, gather_z, gather_x, gather_core, finish]


GRAD_ROWS = 96


def grad_places(second_ref, third_ref, out_ref):
    place = 0
    for ref in (second_ref, third_ref, out_ref):
        for column in range(0, ref.shape[1], LANES):
            for row in range(0, ref.shape[0], 16):
                yield place, ref, column, row
                place += 16


def backward_kernel(
    numbers_ref, owners_ref, grad_ref, packed_ref, out_ref, second_ref, third_ref, last_ref,
    send_ref, recv_ref, send_sem, recv_sem, *reduce_refs,
):
    shards = recv_ref.shape[0]
    barrier = greet_all()
    greet_x(barrier)
    recv_ref[:, CAP:] = jnp.zeros((shards, LANES - CAP, LANES), BF)
    out_ref[...] = jnp.zeros_like(out_ref)
    pl.semaphore_wait(barrier, LANES - 1 + 3)
    reduce = reduce_steps(packed_ref, (second_ref, third_ref, last_ref), *reduce_refs)

    def send(step):
        flip, place, moves = quad(step)
        partners = [shard_at(flip, move, 1) for move in moves]
        members = []
        for shard in partners:
            square = (LANES, LANES)
            field = jnp.broadcast_to(owners_ref[0, pl.ds(shard, 1)], square).T[:CAP].astype(BF)
            sample = jnp.broadcast_to(owners_ref[1, pl.ds(shard, 1)], square).T[:CAP]
            in_sample = one_hot(iota((CAP, LANES), 1).astype(F32) == sample)
            none = jnp.zeros_like(in_sample)
            members.append(
                jnp.concatenate(
                    [
                        jnp.where(field == jnp.array(tile + 1.0, BF), in_sample, none)
                        for tile in range(FIELDS)
                    ],
                    axis=1,
                )
            )
        members = jnp.concatenate(members, axis=0)
        spread = jnp.dot(members, grad_ref[...], preferred_element_type=F32).astype(BF)
        for which, shard in enumerate(partners):
            send_ref[shard] = spread[which * CAP : (which + 1) * CAP]
            send_block(step, which, flip, place, shard, send_ref, recv_ref, send_sem, recv_sem)

    def receive(step):
        flip, _, moves = quad(step)
        wait_for(send_ref.at[pl.ds(0, 4)], recv_sem.at[step])
        partners = [shard_at(flip, move, -1) for move in moves]
        arrived = jnp.concatenate([recv_ref[shard] for shard in partners], axis=0)
        high, low = number_rows(numbers_ref, partners)
        counts = count_rows(high, low, out_ref.shape[0] // LANES)
        out_ref[...] += jnp.dot(counts, arrived, preferred_element_type=F32)

    reduce[0]()
    paced_exchange(
        send,
        receive,
        [
            (2, reduce[1]),
            (10, reduce[2]),
            (16, reduce[3]),
            (21, reduce[4]),
            (26, reduce[5]),
            (34, reduce[6]),
        ],
    )
    reduce[7]()
    wait_for(send_ref.at[pl.ds(0, LANES - 1)], send_sem)


PARAMS = pltpu.CompilerParams(vmem_limit_bytes=48 << 20)


def remote_params(collective_id):
    return pltpu.CompilerParams(
        vmem_limit_bytes=48 << 20, collective_id=collective_id, has_side_effects=True
    )


WHOLE = pl.BlockSpec(memory_space=pltpu.VMEM)


def cost(flops, bytes_accessed):
    return pl.CostEstimate(flops=flops, bytes_accessed=bytes_accessed, transcendentals=0)


def per_device(
    table_rows,
    piece_ids,
    piece_counts,
    piece_dest,
    piece_target,
    labels,
    w_first,
    w_second,
    w_third,
    w_out,
):
    shards = lax.axis_size("emb")
    pieces = piece_ids.shape[0]
    touched, width = table_rows.shape
    samples = labels.shape[0]
    h1, h2 = w_second.shape
    h3 = w_third.shape[1]
    slots = shards * CAP

    blocks = h1 // LANES
    shard = jnp.pad(w_first, ((0, PAD_ROWS - SHARD_ROWS), (0, 0)))
    shard = shard.reshape(PAD_ROWS, blocks, LANES).transpose(1, 0, 2)
    numbers = pl.pallas_call(
        slots_kernel,
        out_shape=jax.ShapeDtypeStruct((10, shards, LANES), F32),
        in_specs=[WHOLE] * 4,
        out_specs=WHOLE,
        compiler_params=PARAMS,
        cost_estimate=cost(2 * 1664 * pieces * LANES, 2_000_000),
    )(
        piece_dest.reshape(1, pieces),
        piece_target.reshape(1, pieces),
        piece_counts.reshape(1, pieces),
        piece_ids.T,
    )
    exchange = [
        pltpu.VMEM((shards, CAP, width), BF),
        pltpu.VMEM((shards, LANES, width), BF),
    ]
    features, owners, full = pl.pallas_call(
        forward_kernel,
        out_shape=(
            jax.ShapeDtypeStruct((samples, FIELDS * width), BF),
            jax.ShapeDtypeStruct((2, shards, LANES), F32),
            jax.ShapeDtypeStruct((blocks, 8, 8, 2, PAD_ROWS, LANES), BF),
        ),
        in_specs=[WHOLE] * 3,
        out_specs=(WHOLE,) * 3,
        scratch_shapes=exchange
        + [
            pltpu.VMEM((FIELDS, samples, width), F32),
            pltpu.SemaphoreType.DMA,
            pltpu.SemaphoreType.DMA((STEPS,)),
            pltpu.SemaphoreType.DMA((6,)),
            pltpu.SemaphoreType.DMA((8,)),
        ],
        compiler_params=remote_params(0),
        cost_estimate=cost(2 * slots * FIELDS * samples * width, 200_000_000),
    )(numbers, table_rows, shard)
    full = full.reshape(blocks, shards * PAD_ROWS, LANES)
    feature_grad, packed = pl.pallas_call(
        dense_kernel,
        out_shape=(
            jax.ShapeDtypeStruct((FIELDS * samples, width), BF),
            jax.ShapeDtypeStruct((64 * GRAD_ROWS, LANES), F32),
        ),
        in_specs=[WHOLE] * 6,
        out_specs=(WHOLE,) * 2,
        scratch_shapes=[
            pltpu.VMEM((samples, shards * PAD_ROWS), BF),
            pltpu.VMEM((FIELDS, samples, width), F32),
        ],
        compiler_params=PARAMS,
        cost_estimate=cost(6 * samples * shards * PAD_ROWS * h1, 16_000_000),
    )(features, labels.reshape(samples, 1), full, w_second, w_third, w_out.reshape(1, h3))
    part = (GRAD_ROWS, LANES)
    row_grad, grad_second, grad_third, grad_out = pl.pallas_call(
        backward_kernel,
        out_shape=(
            jax.ShapeDtypeStruct((touched, width), F32),
            jax.ShapeDtypeStruct((h1, h2), F32),
            jax.ShapeDtypeStruct((h2, h3), F32),
            jax.ShapeDtypeStruct((16, h3), F32),
        ),
        in_specs=[WHOLE] * 4,
        out_specs=(WHOLE,) * 4,
        scratch_shapes=exchange
        + [
            pltpu.SemaphoreType.DMA,
            pltpu.SemaphoreType.DMA((STEPS,)),
            pltpu.VMEM((2, 4, 8) + part, BF),
            pltpu.VMEM((4, 8) + part, F32),
            pltpu.VMEM((4, 8) + part, F32),
            pltpu.VMEM((8,) + part, BF),
            pltpu.VMEM((8,) + part, BF),
            pltpu.VMEM((4, 8) + part, F32),
            pltpu.VMEM((8,) + part, BF),
            pltpu.VMEM(part, BF),
            pltpu.SemaphoreType.DMA((7,)),
            pltpu.SemaphoreType.DMA((7,)),
        ],
        compiler_params=remote_params(1),
        cost_estimate=cost(2 * slots * FIELDS * samples * width, 200_000_000),
    )(numbers, owners, feature_grad, packed.reshape((2, 4, 8) + part))
    return (row_grad, grad_second, grad_third, grad_out[0])


def solution(mesh):
    in_specs = (
        P(("emb", "dp"), None),
        P(("emb", "dp"), None),
        P(("emb", "dp")),
        P(("emb", "dp"), None),
        P(("emb", "dp")),
        P(("emb", "dp")),
        P("emb", None),
        P(),
        P(),
        P(),
    )
    out_specs = (P(("emb", "dp"), None), P(), P(), P())
    return jax.shard_map(
        per_device, mesh=mesh, in_specs=in_specs, out_specs=out_specs, check_vma=False
    )
```

```python
import jax
import jax.numpy as jnp
from jax import lax
from jax.experimental import pallas as pl
from jax.experimental.pallas import tpu as pltpu
from jax.sharding import PartitionSpec as P

FIELDS = 26
LANES = 128
CAP = 80
PIECE_CHUNK = 384
SHARD_ROWS = 26
PAD_ROWS = 32

BF = jnp.bfloat16
F32 = jnp.float32

coef = 0.7978845608028654


def act_slope(values):
    inner = coef * (values + 0.044715 * values * values * values)
    tangent = jnp.tanh(inner)
    result = 0.5 * values * (1.0 + tangent)
    slope = 0.5 * (1.0 + tangent) + 0.5 * values * (1.0 - tangent * tangent) * coef * (
        1.0 + 3.0 * 0.044715 * values * values
    )
    return (result, slope)


def contract(left, right, left_dim, right_dim):
    return lax.dot_general(
        left, right, (((left_dim,), (right_dim,)), ((), ())), preferred_element_type=F32
    )


def iota(shape, dim):
    return lax.broadcasted_iota(jnp.int32, shape, dim)


def one_hot(condition):
    return jnp.where(condition, 1.0, 0.0).astype(BF)


def fill_slots(dest_ref, target_ref, count_ref, ids_ref, slots_ref):
    pieces = dest_ref.shape[1]
    shards = slots_ref.shape[1]
    chunk = PIECE_CHUNK
    before = one_hot(iota((chunk, chunk), 0) < iota((chunk, chunk), 1))
    carry = jnp.zeros((shards, 1), F32)
    total = None
    for step in range(pieces // chunk):
        part = slice(step * chunk, (step + 1) * chunk)
        is_dest = jnp.where(iota((shards, chunk), 0) == dest_ref[:, part], 1.0, 0.0)
        to_dest = is_dest.astype(BF)
        earlier = contract(to_dest, before, 1, 0) + carry
        rank = jnp.sum(is_dest * earlier, axis=0, keepdims=True)
        carry = carry + jnp.sum(is_dest, axis=1, keepdims=True)
        at_rank = one_hot(iota((LANES, chunk), 0).astype(F32) == rank)
        target = target_ref[:, part]
        sample = (target * 2521) >> 16
        field = target - sample * FIELDS
        count = count_ref[:, part]
        numbers = [field + 1, sample]
        for column in range(ids_ref.shape[0]):
            ids = ids_ref[column : column + 1, part]
            numbers.append(jnp.where(column < count, (ids >> 7) + 1, 0))
            numbers.append(ids & (LANES - 1))
        scaled = jnp.concatenate(
            [to_dest * number.astype(F32).astype(BF) for number in numbers], axis=0
        )
        placed = contract(scaled, at_rank, 1, 1)
        total = placed if total is None else total + placed
    for column in range(slots_ref.shape[0]):
        slots_ref[column] = total[column * shards : (column + 1) * shards]


def count_rows(high, low, height):
    slots = low[0].shape[1]
    lows = [one_hot(iota((LANES, slots), 0).astype(F32) == row) for row in low]
    tiles = []
    for tile in range(height):
        parts = [one * one_hot(row == tile + 1.0) for one, row in zip(lows, high)]
        tiles.append((parts[0] + parts[1]) + (parts[2] + parts[3]))
    return jnp.concatenate(tiles, axis=0)


def number_rows(numbers_ref, shards):
    def row(column):
        return jnp.concatenate([numbers_ref[column, pl.ds(one, 1)] for one in shards], axis=1)

    return [row(2 + 2 * k) for k in range(4)], [row(3 + 2 * k) for k in range(4)]


STEPS = 32
LAG = 10


def quad(step):
    flip = step % 2
    place = (step // 2 * 7 + 2) % 16
    a, b = 1 + place // 4, place % 4
    last = 4 * ((place // 12) * ((4 - b) // 4))
    return flip, place, ((a, b), (8 - b, a), (8 + last - a, 8 - b), (b + last, 8 - a))


def shard_at(flip, move, sign):
    emb = lax.axis_index("emb")
    z = (emb // 16 + 8 + sign * move[0]) % 8
    y = ((emb // 2) % 8 + 8 + sign * move[1]) % 8
    return z * 16 + y * 2 + (emb + flip) % 2


def greet_all():
    emb = lax.axis_index("emb")
    barrier = pltpu.get_barrier_semaphore()

    def greet(step, carry):
        pl.semaphore_signal(
            barrier,
            inc=1,
            device_id={"emb": (emb + step) % LANES},
            device_id_type=pl.DeviceIdType.MESH,
        )
        return carry

    lax.fori_loop(1, LANES, greet, 0)
    return barrier


def send_block(step, which, flip, place, shard, send_ref, recv_ref, send_sem, recv_sem):
    emb = lax.axis_index("emb")
    source = send_ref.at[shard]
    target = recv_ref.at[emb, pl.ds(0, CAP)]

    def away():
        send_to({"emb": shard}, source, target, send_sem, recv_sem.at[step])

    if which != 2:
        away()
        return
    own = (place == 12) & (flip == 0)

    @pl.when(own)
    def _():
        pltpu.make_async_copy(source, target, recv_sem.at[step]).start()

    @pl.when(jnp.logical_not(own))
    def _():
        away()


def gather_steps(shard_ref, full_ref, send_sem, recv_sem):
    emb, x = lax.axis_index("emb"), lax.axis_index("dp")
    z, y, core = emb // 16, (emb // 2) % 8, emb % 2
    other = device(core=1 - core)
    first, second = 2 * x, 2 * x + 1

    def start():
        for block in (first, second):
            full_ref[block, z, y, core] = shard_ref[block]
        for step in range(1, 8):
            mine = full_ref.at[first, z, y, core]
            send_to(device(z=(z + step) % 8), mine, mine, send_sem.at[0], recv_sem.at[0])
            mine = full_ref.at[second, z, y, core]
            send_to(device(y=(y + step) % 8), mine, mine, send_sem.at[1], recv_sem.at[1])

    def lines():
        wait_for(full_ref.at[first, pl.ds(0, 7), y, core], recv_sem.at[0])
        wait_for(full_ref.at[second, z, pl.ds(0, 7), core], recv_sem.at[1])
        for step in range(1, 8):
            mine = full_ref.at[first, :, y, core]
            send_to(device(y=(y + step) % 8), mine, mine, send_sem.at[2], recv_sem.at[2])
            mine = full_ref.at[second, z, :, core]
            send_to(device(z=(z + step) % 8), mine, mine, send_sem.at[3], recv_sem.at[3])

    def over_x():
        wait_for(full_ref.at[first, :, pl.ds(0, 7), core], recv_sem.at[2])
        wait_for(full_ref.at[second, pl.ds(0, 7), :, core], recv_sem.at[3])
        mine = full_ref.at[pl.ds(first, 2), :, :, core]
        for step in range(1, 4):
            send_to(device(x=(x + step) % 4), mine, mine, send_sem.at[4], recv_sem.at[3 + step])
        send_to(other, mine, mine, send_sem.at[5], recv_sem.at[7])

    def over_core(step):
        def forward():
            mine = full_ref.at[pl.ds(2 * ((x + 4 - step) % 4), 2), :, :, core]
            wait_for(mine, recv_sem.at[3 + step])
            send_to(other, mine, mine, send_sem.at[5], recv_sem.at[7])

        return forward

    def finish():
        wait_for(full_ref.at[:, :, :, core], recv_sem.at[7])
        wait_for(full_ref.at[first, pl.ds(0, 7), y, core], send_sem.at[0])
        wait_for(full_ref.at[second, z, pl.ds(0, 7), core], send_sem.at[1])
        wait_for(full_ref.at[first, :, pl.ds(0, 7), core], send_sem.at[2])
        wait_for(full_ref.at[second, pl.ds(0, 7), :, core], send_sem.at[3])
        wait_for(full_ref.at[pl.ds(0, 6), :, :, core], send_sem.at[4])
        wait_for(full_ref.at[:, :, :, core], send_sem.at[5])

    return [start, lines, over_x, over_core(1), over_core(3), over_core(2), finish]


def greet_x(barrier):
    x = lax.axis_index("dp")
    for step in range(1, 4):
        pl.semaphore_signal(
            barrier,
            inc=1,
            device_id=device(x=(x + step) % 4),
            device_id_type=pl.DeviceIdType.MESH,
        )


def paced_exchange(send, receive, others):
    def one(step, carry):
        for at, other in others:
            pl.when(step == at)(other)

        @pl.when(step < STEPS)
        def _():
            send(step)

        @pl.when(step >= LAG)
        def _():
            receive(step - LAG)

        return carry

    lax.fori_loop(0, STEPS + LAG, one, 0)


def step_kernel(
    dest_ref, target_ref, count_ref, ids_ref, rows_ref, shard_ref, label_ref, second_ref,
    third_ref, last_ref,
    row_grad_ref, grad_second_ref, grad_third_ref, grad_out_ref,
    numbers_ref, owners_ref, full_ref, feature_ref, grad_ref, packed_ref, padded_ref, sums_ref,
    send_ref, recv_ref, back_ref, send_sem, recv_sem, back_send_sem, back_recv_sem,
    gather_send, gather_recv, *reduce_refs,
):
    gather = gather_steps(shard_ref, full_ref, gather_send, gather_recv)
    outs = (grad_second_ref, grad_third_ref, grad_out_ref)
    reduce = reduce_steps(packed_ref, outs, *reduce_refs)
    barrier = greet_all()
    greet_x(barrier)
    empty = jnp.zeros((recv_ref.shape[0], LANES - CAP, LANES), BF)
    recv_ref[:, CAP:] = empty
    back_ref[:, CAP:] = empty
    sums_ref[...] = jnp.zeros_like(sums_ref)
    row_grad_ref[...] = jnp.zeros_like(row_grad_ref)
    fill_slots(dest_ref, target_ref, count_ref, ids_ref, numbers_ref)
    pl.semaphore_wait(barrier, LANES - 1 + 3)
    gather[0]()
    forward_exchange(
        numbers_ref, rows_ref, feature_ref, owners_ref, send_ref, recv_ref, sums_ref,
        send_sem, recv_sem, gather,
    )
    dense_step(
        feature_ref, label_ref, full_ref, second_ref, third_ref, last_ref,
        grad_ref, packed_ref, padded_ref, sums_ref, reduce[0],
    )
    backward_exchange(
        numbers_ref, owners_ref, grad_ref, row_grad_ref, send_ref, back_ref,
        back_send_sem, back_recv_sem, reduce,
    )


def forward_exchange(
    numbers_ref, rows_ref, out_ref, owners_ref, send_ref, recv_ref, sums_ref,
    send_sem, recv_sem, gather,
):
    def send(step):
        flip, place, moves = quad(step)
        for which, move in enumerate(moves):
            shard = shard_at(flip, move, 1)
            high, low = number_rows(numbers_ref, [shard])
            counts = count_rows(high, low, rows_ref.shape[0] // LANES)
            pooled = contract(counts, rows_ref[...], 0, 0)[:CAP]
            end = iota((8, LANES), 0)
            tail = jnp.where(end == 6, numbers_ref[0, pl.ds(shard, 1)], pooled[CAP - 8 :])
            tail = jnp.where(end == 7, numbers_ref[1, pl.ds(shard, 1)], tail)
            send_ref[shard] = jnp.concatenate([pooled[: CAP - 8], tail], axis=0).astype(BF)
            send_block(step, which, flip, place, shard, send_ref, recv_ref, send_sem, recv_sem)

    def receive(step):
        flip, _, moves = quad(step)
        wait_for(send_ref.at[pl.ds(0, 4)], recv_sem.at[step])
        arrived, fields, samples = [], [], []
        for move in moves:
            shard = shard_at(flip, move, -1)
            block = recv_ref[shard]
            tail = block[CAP - 16 : CAP].astype(F32)
            arrived.append(block)
            fields.append(tail[14:15])
            samples.append(tail[15:16])
            owners_ref[0, pl.ds(shard, 1)] = fields[-1]
            owners_ref[1, pl.ds(shard, 1)] = samples[-1]
        arrived = jnp.concatenate(arrived, axis=0)
        field = jnp.concatenate(fields, axis=1)
        sample = jnp.concatenate(samples, axis=1)
        in_sample = one_hot(iota((LANES, 4 * LANES), 0).astype(F32) == sample)
        for tile in range(FIELDS):
            member = in_sample * one_hot(field == tile + 1.0)
            sums_ref[tile] += jnp.dot(member, arrived, preferred_element_type=F32)

    paced_exchange(
        send,
        receive,
        [(1, gather[1]), (8, gather[2]), (32, gather[3]), (34, gather[4]), (38, gather[5])],
    )
    wait_for(send_ref.at[pl.ds(0, LANES - 1)], send_sem)
    for tile in range(FIELDS):
        out_ref[:, tile * LANES : (tile + 1) * LANES] = sums_ref[tile].astype(BF)
    gather[6]()


def window_tile(tile):
    start = tile * 4 * SHARD_ROWS
    return min(start // LANES, FIELDS - 2), start


def window_map(tile):
    first, start = window_tile(tile)
    feature = iota((2 * LANES, LANES), 0) + (first * LANES - start)
    place = iota((2 * LANES, LANES), 1)
    row = place % PAD_ROWS
    wanted = (place // PAD_ROWS) * SHARD_ROWS + row
    return jnp.where(row < SHARD_ROWS, one_hot(feature == wanted), jnp.zeros((), BF))


def dense_step(
    feature_ref, label_ref, first_ref, second_ref, third_ref, last_ref,
    grad_ref, packed_ref, padded_ref, network_ref, after_sums,
):
    blocks, padded_rows = first_ref.shape[0], padded_ref.shape[1]
    padded_tiles = padded_rows // LANES
    for tile in range(padded_tiles):
        first, _ = window_tile(tile)
        window = feature_ref[:, first * LANES : (first + 2) * LANES]
        padded = jnp.dot(window, window_map(tile), preferred_element_type=F32)
        padded_ref[:, tile * LANES : (tile + 1) * LANES] = padded.astype(BF)
    first_pre = jnp.concatenate(
        [
            jnp.dot(
                padded_ref[...],
                first_ref[block].reshape(padded_rows, LANES),
                preferred_element_type=F32,
            )
            for block in range(blocks)
        ],
        axis=1,
    )
    first_act, first_slope = act_slope(first_pre)
    first_act = first_act.astype(BF)
    second_act, second_slope = act_slope(
        jnp.dot(first_act, second_ref[...], preferred_element_type=F32)
    )
    second_act = second_act.astype(BF)
    third_act, third_slope = act_slope(
        jnp.dot(second_act, third_ref[...], preferred_element_type=F32)
    )
    third_act = third_act.astype(BF).astype(F32)
    last = last_ref[...].astype(F32)
    deep = jnp.sum(third_act * last, axis=1, keepdims=True)
    total = jnp.zeros((feature_ref.shape[0], LANES), F32)
    squares = jnp.zeros((feature_ref.shape[0], LANES), F32)
    for tile in range(FIELDS):
        vector = feature_ref[:, tile * LANES : (tile + 1) * LANES].astype(F32)
        total = total + vector
        squares = squares + vector * vector
    pairs = 0.5 * jnp.sum(total * total - squares, axis=1, keepdims=True)
    logit_grad = jax.nn.sigmoid(deep + pairs) - label_ref[...].astype(F32)
    h1, h2 = second_ref.shape
    h3 = third_ref.shape[1]
    start = h1 * h2 // LANES
    end = start + h2 * h3 // LANES
    packed_ref[end:] = jnp.zeros_like(packed_ref[end:])
    grad_out = jnp.sum(logit_grad * third_act, axis=0, keepdims=True)
    for tile in range(h3 // LANES):
        packed_ref[end + 16 * tile : end + 16 * tile + 1] = grad_out[
            :, tile * LANES : (tile + 1) * LANES
        ]
    third_grad = (logit_grad * last * third_slope).astype(BF)
    grad_third = contract(second_act, third_grad, 0, 0)
    for tile in range(h3 // LANES):
        packed_ref[start + tile * h2 : start + (tile + 1) * h2] = grad_third[
            :, tile * LANES : (tile + 1) * LANES
        ]
    second_grad = (contract(third_grad, third_ref[...], 1, 1) * second_slope).astype(BF)
    for tile in range(h2 // LANES):
        packed_ref[tile * h1 : (tile + 1) * h1] = contract(
            first_act, second_grad[:, tile * LANES : (tile + 1) * LANES], 0, 0
        )
    after_sums()
    first_grad = (contract(second_grad, second_ref[...], 1, 1) * first_slope).astype(BF)
    network_ref[...] = jnp.zeros_like(network_ref)
    for tile in range(padded_tiles):
        first, _ = window_tile(tile)
        z, y = tile // 4, tile % 4 * 2
        weights = [first_ref[block, z, y : y + 2] for block in range(blocks)]
        weights = jnp.concatenate([one.reshape(LANES, LANES) for one in weights], axis=1)
        part = contract(first_grad, weights, 1, 1)
        upper = part.astype(BF)
        lower = (part - upper.astype(F32)).astype(BF)
        place = window_map(tile)
        moved = contract(upper, place, 1, 1) + contract(lower, place, 1, 1)
        network_ref[first] += moved[:, :LANES]
        network_ref[first + 1] += moved[:, LANES:]
    for tile in range(FIELDS):
        vector = feature_ref[:, tile * LANES : (tile + 1) * LANES].astype(F32)
        grad_ref[tile * LANES : (tile + 1) * LANES] = (
            network_ref[tile] + logit_grad * (total - vector)
        ).astype(BF)


def device(**axes):
    emb, dp = lax.axis_index("emb"), lax.axis_index("dp")
    z, y, core = emb // 16, (emb // 2) % 8, emb % 2
    z, y, core = axes.get("z", z), axes.get("y", y), axes.get("core", core)
    return {"emb": z * 16 + y * 2 + core, "dp": axes.get("x", dp)}


def send_to(partner, source, target, send_sem, recv_sem):
    pltpu.make_async_remote_copy(
        source,
        target,
        send_sem,
        recv_sem,
        device_id=partner,
        device_id_type=pl.DeviceIdType.MESH,
    ).start()


def wait_for(block, sem):
    pltpu.make_async_copy(block, block, sem).wait()


def reduce_steps(
    packed_ref, outs, full_ref, from_core, from_x, from_z, from_y, sum_core, sum_x, sum_z,
    send_sem, recv_sem,
):
    emb, x = lax.axis_index("emb"), lax.axis_index("dp")
    z, y, core = emb // 16, (emb // 2) % 8, emb % 2
    other = device(core=1 - core)
    half = packed_ref.shape[0] // 2
    eighth = half // 4

    def over_core():
        theirs = packed_ref.at[pl.ds(pl.multiple_of((1 - core) * half, eighth), half)]
        send_to(other, theirs, from_core, send_sem.at[0], recv_sem.at[0])

    def over_x():
        wait_for(from_core, recv_sem.at[0])
        for part in range(4):
            mine = packed_ref[pl.ds(pl.multiple_of(core * half + part * eighth, eighth), eighth)]
            theirs = from_core[part * eighth : (part + 1) * eighth]
            sum_core[part] = (mine + theirs).reshape(sum_core.shape[1:])
        for step in range(1, 4):
            to = (x + step) % 4
            send_to(device(x=to), sum_core.at[to], from_x.at[x], send_sem.at[1], recv_sem.at[1])
        from_x[x] = sum_core[x]

    def over_z():
        wait_for(from_x.at[pl.ds(0, 3)], recv_sem.at[1])
        for part in range(8):
            total = (from_x[0, part] + from_x[1, part]) + (from_x[2, part] + from_x[3, part])
            sum_x[part] = total.astype(BF)
        for step in range(1, 8):
            to = (z + step) % 8
            send_to(device(z=to), sum_x.at[to], from_z.at[z], send_sem.at[2], recv_sem.at[2])
        from_z[z] = sum_x[z]

    def over_y():
        wait_for(from_z.at[pl.ds(0, 7)], recv_sem.at[2])
        sum_z[...] = jnp.sum(from_z[...].astype(F32), axis=0).astype(BF)
        for step in range(1, 8):
            to = (y + step) % 8
            send_to(device(y=to), sum_z, from_y.at[y], send_sem.at[3], recv_sem.at[3])
        from_y[y] = sum_z[...]

    def gather_z():
        wait_for(from_y.at[pl.ds(0, 7)], recv_sem.at[3])
        full_ref[core, x, z] = jnp.sum(from_y[...].astype(F32), axis=0).astype(BF)
        mine = full_ref.at[core, x, z]
        for step in range(1, 8):
            send_to(device(z=(z + step) % 8), mine, mine, send_sem.at[4], recv_sem.at[4])

    def gather_x():
        wait_for(full_ref.at[core, x, pl.ds(0, 7)], recv_sem.at[4])
        mine = full_ref.at[core, x]
        for step in range(1, 4):
            send_to(device(x=(x + step) % 4), mine, mine, send_sem.at[5], recv_sem.at[5])

    def gather_core():
        wait_for(full_ref.at[core, pl.ds(0, 3)], recv_sem.at[5])
        mine = full_ref.at[core]
        send_to(other, mine, mine, send_sem.at[6], recv_sem.at[6])

    def finish():
        wait_for(full_ref.at[0], recv_sem.at[6])
        wait_for(from_core, send_sem.at[0])
        wait_for(from_x.at[pl.ds(0, 3)], send_sem.at[1])
        wait_for(from_z.at[pl.ds(0, 7)], send_sem.at[2])
        wait_for(from_y.at[pl.ds(0, 7)], send_sem.at[3])
        wait_for(full_ref.at[core, x, pl.ds(0, 7)], send_sem.at[4])
        wait_for(full_ref.at[core, pl.ds(0, 3)], send_sem.at[5])
        wait_for(full_ref.at[0], send_sem.at[6])
        for place, ref, column, row in grad_places(*outs):
            half, place = divmod(place, 4 * 8 * GRAD_ROWS)
            quarter, place = divmod(place, 8 * GRAD_ROWS)
            part, inside = divmod(place, GRAD_ROWS)
            block = full_ref[half, quarter, part, inside : inside + 16]
            ref[row : row + 16, column : column + LANES] = block.astype(F32)

    return [over_core, over_x, over_z, over_y, gather_z, gather_x, gather_core, finish]


GRAD_ROWS = 96


def grad_places(second_ref, third_ref, out_ref):
    place = 0
    for ref in (second_ref, third_ref, out_ref):
        for column in range(0, ref.shape[1], LANES):
            for row in range(0, ref.shape[0], 16):
                yield place, ref, column, row
                place += 16


def backward_exchange(
    numbers_ref, owners_ref, grad_ref, out_ref, send_ref, recv_ref, send_sem, recv_sem, reduce
):
    def send(step):
        flip, place, moves = quad(step)
        partners = [shard_at(flip, move, 1) for move in moves]
        members = []
        for shard in partners:
            square = (LANES, LANES)
            field = jnp.broadcast_to(owners_ref[0, pl.ds(shard, 1)], square).T[:CAP].astype(BF)
            sample = jnp.broadcast_to(owners_ref[1, pl.ds(shard, 1)], square).T[:CAP]
            in_sample = one_hot(iota((CAP, LANES), 1).astype(F32) == sample)
            none = jnp.zeros_like(in_sample)
            members.append(
                jnp.concatenate(
                    [
                        jnp.where(field == jnp.array(tile + 1.0, BF), in_sample, none)
                        for tile in range(FIELDS)
                    ],
                    axis=1,
                )
            )
        members = jnp.concatenate(members, axis=0)
        spread = jnp.dot(members, grad_ref[...], preferred_element_type=F32).astype(BF)
        for which, shard in enumerate(partners):
            send_ref[shard] = spread[which * CAP : (which + 1) * CAP]
            send_block(step, which, flip, place, shard, send_ref, recv_ref, send_sem, recv_sem)

    def receive(step):
        flip, _, moves = quad(step)
        wait_for(send_ref.at[pl.ds(0, 4)], recv_sem.at[step])
        partners = [shard_at(flip, move, -1) for move in moves]
        arrived = jnp.concatenate([recv_ref[shard] for shard in partners], axis=0)
        high, low = number_rows(numbers_ref, partners)
        counts = count_rows(high, low, out_ref.shape[0] // LANES)
        out_ref[...] += jnp.dot(counts, arrived, preferred_element_type=F32)

    paced_exchange(
        send,
        receive,
        [
            (2, reduce[1]),
            (10, reduce[2]),
            (16, reduce[3]),
            (21, reduce[4]),
            (26, reduce[5]),
            (34, reduce[6]),
        ],
    )
    reduce[7]()
    wait_for(send_ref.at[pl.ds(0, LANES - 1)], send_sem)


def remote_params(collective_id):
    return pltpu.CompilerParams(
        vmem_limit_bytes=56 << 20, collective_id=collective_id, has_side_effects=True
    )


WHOLE = pl.BlockSpec(memory_space=pltpu.VMEM)


def cost(flops, bytes_accessed):
    return pl.CostEstimate(flops=flops, bytes_accessed=bytes_accessed, transcendentals=0)


def per_device(
    table_rows,
    piece_ids,
    piece_counts,
    piece_dest,
    piece_target,
    labels,
    w_first,
    w_second,
    w_third,
    w_out,
):
    shards = lax.axis_size("emb")
    pieces = piece_ids.shape[0]
    touched, width = table_rows.shape
    samples = labels.shape[0]
    h1, h2 = w_second.shape
    h3 = w_third.shape[1]

    blocks = h1 // LANES
    padded = shards * PAD_ROWS
    shard = jnp.pad(w_first, ((0, PAD_ROWS - SHARD_ROWS), (0, 0)))
    shard = shard.reshape(PAD_ROWS, blocks, LANES).transpose(1, 0, 2)
    part = (GRAD_ROWS, LANES)
    row_grad, grad_second, grad_third, grad_out = pl.pallas_call(
        step_kernel,
        out_shape=(
            jax.ShapeDtypeStruct((touched, width), F32),
            jax.ShapeDtypeStruct((h1, h2), F32),
            jax.ShapeDtypeStruct((h2, h3), F32),
            jax.ShapeDtypeStruct((16, h3), F32),
        ),
        in_specs=[WHOLE] * 10,
        out_specs=(WHOLE,) * 4,
        scratch_shapes=[
            pltpu.VMEM((10, shards, LANES), F32),
            pltpu.VMEM((2, shards, LANES), F32),
            pltpu.VMEM((blocks, 8, 8, 2, PAD_ROWS, LANES), BF),
            pltpu.VMEM((samples, FIELDS * width), BF),
            pltpu.VMEM((FIELDS * samples, width), BF),
            pltpu.VMEM((64 * GRAD_ROWS, LANES), F32),
            pltpu.VMEM((samples, padded), BF),
            pltpu.VMEM((FIELDS, samples, width), F32),
            pltpu.VMEM((shards, CAP, width), BF),
            pltpu.VMEM((shards, LANES, width), BF),
            pltpu.VMEM((shards, LANES, width), BF),
            pltpu.SemaphoreType.DMA,
            pltpu.SemaphoreType.DMA((STEPS,)),
            pltpu.SemaphoreType.DMA,
            pltpu.SemaphoreType.DMA((STEPS,)),
            pltpu.SemaphoreType.DMA((6,)),
            pltpu.SemaphoreType.DMA((8,)),
            pltpu.VMEM((2, 4, 8) + part, BF),
            pltpu.VMEM((32 * GRAD_ROWS, LANES), F32),
            pltpu.VMEM((4, 8) + part, F32),
            pltpu.VMEM((8,) + part, BF),
            pltpu.VMEM((8,) + part, BF),
            pltpu.VMEM((4, 8) + part, F32),
            pltpu.VMEM((8,) + part, BF),
            pltpu.VMEM(part, BF),
            pltpu.SemaphoreType.DMA((7,)),
            pltpu.SemaphoreType.DMA((7,)),
        ],
        compiler_params=remote_params(0),
        cost_estimate=cost(4 * shards * CAP * FIELDS * samples * width, 400_000_000),
    )(
        piece_dest.reshape(1, pieces),
        piece_target.reshape(1, pieces),
        piece_counts.reshape(1, pieces),
        piece_ids.T,
        table_rows,
        shard,
        labels.reshape(samples, 1),
        w_second,
        w_third,
        w_out.reshape(1, h3),
    )
    return (row_grad, grad_second, grad_third, grad_out[0])


def solution(mesh):
    in_specs = (
        P(("emb", "dp"), None),
        P(("emb", "dp"), None),
        P(("emb", "dp")),
        P(("emb", "dp"), None),
        P(("emb", "dp")),
        P(("emb", "dp")),
        P("emb", None),
        P(),
        P(),
        P(),
    )
    out_specs = (P(("emb", "dp"), None), P(), P(), P())
    return jax.shard_map(
        per_device, mesh=mesh, in_specs=in_specs, out_specs=out_specs, check_vma=False
    )
```

```python
import jax
import jax.numpy as jnp
from jax import lax
from jax.experimental import pallas as pl
from jax.experimental.pallas import tpu as pltpu
from jax.sharding import PartitionSpec as P

FIELDS = 26
LANES = 128
CAP = 80
PIECE_CHUNK = 384
SHARD_ROWS = 26
PAD_ROWS = 32

BF = jnp.bfloat16
F32 = jnp.float32

coef = 0.7978845608028654


def act_slope(values):
    inner = coef * (values + 0.044715 * values * values * values)
    tangent = jnp.tanh(inner)
    result = 0.5 * values * (1.0 + tangent)
    slope = 0.5 * (1.0 + tangent) + 0.5 * values * (1.0 - tangent * tangent) * coef * (
        1.0 + 3.0 * 0.044715 * values * values
    )
    return (result, slope)


def contract(left, right, left_dim, right_dim):
    return lax.dot_general(
        left, right, (((left_dim,), (right_dim,)), ((), ())), preferred_element_type=F32
    )


def iota(shape, dim):
    return lax.broadcasted_iota(jnp.int32, shape, dim)


def one_hot(condition):
    return jnp.where(condition, 1.0, 0.0).astype(BF)


def flat_part(ref, step):
    rows = range(step * PIECE_CHUNK // LANES, (step + 1) * PIECE_CHUNK // LANES)
    return jnp.concatenate([ref[row : row + 1] for row in rows], axis=1)


def fill_slots(dest_ref, target_ref, count_ref, ids_ref, slots_ref):
    pieces = dest_ref.shape[1]
    shards = slots_ref.shape[1]
    chunk = PIECE_CHUNK
    before = one_hot(iota((chunk, chunk), 0) < iota((chunk, chunk), 1))
    carry = jnp.zeros((shards, 1), F32)
    total = None
    for step in range(pieces // chunk):
        part = slice(step * chunk, (step + 1) * chunk)
        is_dest = jnp.where(iota((shards, chunk), 0) == dest_ref[:, part], 1.0, 0.0)
        to_dest = is_dest.astype(BF)
        earlier = contract(to_dest, before, 1, 0) + carry
        rank = jnp.sum(is_dest * earlier, axis=0, keepdims=True)
        carry = carry + jnp.sum(is_dest, axis=1, keepdims=True)
        at_rank = one_hot(iota((LANES, chunk), 0).astype(F32) == rank)
        target = flat_part(target_ref, step)
        sample = (target * 2521) >> 16
        field = target - sample * FIELDS
        count = flat_part(count_ref, step)
        numbers = [field + 1, sample]
        for column in range(ids_ref.shape[0]):
            ids = ids_ref[column : column + 1, part]
            numbers.append(jnp.where(column < count, (ids >> 7) + 1, 0))
            numbers.append(ids & (LANES - 1))
        scaled = jnp.concatenate(
            [to_dest * number.astype(F32).astype(BF) for number in numbers], axis=0
        )
        placed = contract(scaled, at_rank, 1, 1)
        total = placed if total is None else total + placed
    for column in range(slots_ref.shape[0]):
        slots_ref[column] = total[column * shards : (column + 1) * shards]


def count_rows(high, low, height):
    slots = low[0].shape[1]
    lows = [one_hot(iota((LANES, slots), 0).astype(F32) == row) for row in low]
    tiles = []
    for tile in range(height):
        parts = [one * one_hot(row == tile + 1.0) for one, row in zip(lows, high)]
        tiles.append((parts[0] + parts[1]) + (parts[2] + parts[3]))
    return jnp.concatenate(tiles, axis=0)


def number_rows(numbers_ref, shards):
    def row(column):
        return jnp.concatenate([numbers_ref[column, pl.ds(one, 1)] for one in shards], axis=1)

    return [row(2 + 2 * k) for k in range(4)], [row(3 + 2 * k) for k in range(4)]


STEPS = 32
LAG = 12


def quad(step):
    flip = step % 2
    place = (step // 2 * 7 + 2) % 16
    a, b = 1 + place // 4, place % 4
    last = 4 * ((place // 12) * ((4 - b) // 4))
    return flip, place, ((a, b), (8 - b, a), (8 + last - a, 8 - b), (b + last, 8 - a))


def shard_at(flip, move, sign):
    emb = lax.axis_index("emb")
    z = (emb // 16 + 8 + sign * move[0]) % 8
    y = ((emb // 2) % 8 + 8 + sign * move[1]) % 8
    return z * 16 + y * 2 + (emb + flip) % 2


def greet_all():
    emb = lax.axis_index("emb")
    barrier = pltpu.get_barrier_semaphore()

    def greet(step, carry):
        pl.semaphore_signal(
            barrier,
            inc=1,
            device_id={"emb": (emb + step) % LANES},
            device_id_type=pl.DeviceIdType.MESH,
        )
        return carry

    lax.fori_loop(1, LANES, greet, 0)
    return barrier


def send_block(step, which, flip, place, shard, send_ref, recv_ref, send_sem, recv_sem):
    emb = lax.axis_index("emb")
    source = send_ref.at[shard]
    target = recv_ref.at[emb, pl.ds(0, CAP)]

    def away():
        send_to({"emb": shard}, source, target, send_sem, recv_sem.at[step])

    if which != 2:
        away()
        return
    own = (place == 12) & (flip == 0)

    @pl.when(own)
    def _():
        pltpu.make_async_copy(source, target, recv_sem.at[step]).start()

    @pl.when(jnp.logical_not(own))
    def _():
        away()


def gather_steps(shard_ref, full_ref, send_sem, recv_sem):
    emb, x = lax.axis_index("emb"), lax.axis_index("dp")
    z, y, core = emb // 16, (emb // 2) % 8, emb % 2
    other = device(core=1 - core)
    first, second = 2 * x, 2 * x + 1
    right, left = (x + 1) % 4, (x + 3) % 4

    def mine(whose):
        return full_ref.at[pl.ds(2 * whose, 2), :, :, core]

    def start():
        for block in (first, second):
            full_ref[block, z, y, core] = shard_ref[block]
        for step in range(1, 8):
            block_here = full_ref.at[first, z, y, core]
            send_to(device(z=(z + step) % 8), block_here, block_here, send_sem.at[0], recv_sem.at[0])
            block_here = full_ref.at[second, z, y, core]
            send_to(device(y=(y + step) % 8), block_here, block_here, send_sem.at[1], recv_sem.at[1])

    def lines():
        wait_for(full_ref.at[first, pl.ds(0, 7), y, core], recv_sem.at[0])
        wait_for(full_ref.at[second, z, pl.ds(0, 7), core], recv_sem.at[1])
        for step in range(1, 8):
            block_here = full_ref.at[first, :, y, core]
            send_to(device(y=(y + step) % 8), block_here, block_here, send_sem.at[2], recv_sem.at[2])
            block_here = full_ref.at[second, z, :, core]
            send_to(device(z=(z + step) % 8), block_here, block_here, send_sem.at[3], recv_sem.at[3])

    def over_x():
        wait_for(full_ref.at[first, :, pl.ds(0, 7), core], recv_sem.at[2])
        wait_for(full_ref.at[second, pl.ds(0, 7), :, core], recv_sem.at[3])
        send_to(device(x=right), mine(x), mine(x), send_sem.at[4], recv_sem.at[4])
        send_to(device(x=left), mine(x), mine(x), send_sem.at[4], recv_sem.at[5])
        send_to(other, mine(x), mine(x), send_sem.at[5], recv_sem.at[8])

    def forward():
        wait_for(mine(left), recv_sem.at[4])
        block = full_ref.at[2 * left, :, :, core]
        send_to(device(x=right), block, block, send_sem.at[4], recv_sem.at[6])
        wait_for(mine(right), recv_sem.at[5])
        block = full_ref.at[2 * right + 1, :, :, core]
        send_to(device(x=left), block, block, send_sem.at[4], recv_sem.at[7])
        for near in (left, right):
            send_to(other, mine(near), mine(near), send_sem.at[5], recv_sem.at[8])

    def over_core():
        far = (x + 2) % 4
        wait_for(full_ref.at[2 * far, :, :, core], recv_sem.at[6])
        wait_for(full_ref.at[2 * far + 1, :, :, core], recv_sem.at[7])
        send_to(other, mine(far), mine(far), send_sem.at[5], recv_sem.at[8])

    def finish():
        wait_for(full_ref.at[:, :, :, core], recv_sem.at[8])
        wait_for(full_ref.at[first, pl.ds(0, 7), y, core], send_sem.at[0])
        wait_for(full_ref.at[second, z, pl.ds(0, 7), core], send_sem.at[1])
        wait_for(full_ref.at[first, :, pl.ds(0, 7), core], send_sem.at[2])
        wait_for(full_ref.at[second, pl.ds(0, 7), :, core], send_sem.at[3])
        wait_for(full_ref.at[pl.ds(0, 6), :, :, core], send_sem.at[4])
        wait_for(full_ref.at[:, :, :, core], send_sem.at[5])

    return [start, lines, over_x, forward, over_core, finish]


def greet_x(barrier):
    x = lax.axis_index("dp")
    for step in range(1, 4):
        pl.semaphore_signal(
            barrier,
            inc=1,
            device_id=device(x=(x + step) % 4),
            device_id_type=pl.DeviceIdType.MESH,
        )


def paced_exchange(send, receive, others):
    def one(step, carry):
        for at, other in others:
            pl.when(step == at)(other)

        @pl.when(step < STEPS)
        def _():
            send(step)

        @pl.when(step >= LAG)
        def _():
            receive(step - LAG)

        return carry

    lax.fori_loop(0, STEPS + LAG, one, 0)


def step_kernel(
    dest_ref, target_ref, count_ref, ids_ref, rows_ref, shard_ref, label_ref, second_ref,
    third_ref, last_ref,
    row_grad_ref, grad_second_ref, grad_third_ref, grad_out_ref,
    numbers_ref, owners_ref, full_ref, feature_ref, grad_ref, packed_ref, padded_ref, sums_ref,
    send_ref, recv_ref, back_ref, send_sem, recv_sem, back_send_sem, back_recv_sem,
    gather_send, gather_recv, *reduce_refs,
):
    gather = gather_steps(shard_ref, full_ref, gather_send, gather_recv)
    outs = (grad_second_ref, grad_third_ref, grad_out_ref)
    reduce = reduce_steps(packed_ref, outs, *reduce_refs)
    barrier = greet_all()
    greet_x(barrier)
    empty = jnp.zeros((recv_ref.shape[0], LANES - CAP, LANES), BF)
    recv_ref[:, CAP:] = empty
    back_ref[:, CAP:] = empty
    sums_ref[...] = jnp.zeros_like(sums_ref)
    row_grad_ref[...] = jnp.zeros_like(row_grad_ref)
    fill_slots(dest_ref, target_ref, count_ref, ids_ref, numbers_ref)
    pl.semaphore_wait(barrier, LANES - 1 + 3)
    gather[0]()
    forward_exchange(
        numbers_ref, rows_ref, feature_ref, owners_ref, send_ref, recv_ref, sums_ref,
        send_sem, recv_sem, gather,
    )
    dense_step(
        feature_ref, label_ref, full_ref, second_ref, third_ref, last_ref,
        grad_ref, packed_ref, padded_ref, sums_ref, reduce[0],
    )
    backward_exchange(
        numbers_ref, owners_ref, grad_ref, row_grad_ref, send_ref, back_ref,
        back_send_sem, back_recv_sem, reduce,
    )


def forward_exchange(
    numbers_ref, rows_ref, out_ref, owners_ref, send_ref, recv_ref, sums_ref,
    send_sem, recv_sem, gather,
):
    def send(step):
        flip, place, moves = quad(step)
        for which, move in enumerate(moves):
            shard = shard_at(flip, move, 1)
            high, low = number_rows(numbers_ref, [shard])
            counts = count_rows(high, low, rows_ref.shape[0] // LANES)
            pooled = contract(counts, rows_ref[...], 0, 0)[:CAP]
            end = iota((8, LANES), 0)
            tail = jnp.where(end == 6, numbers_ref[0, pl.ds(shard, 1)], pooled[CAP - 8 :])
            tail = jnp.where(end == 7, numbers_ref[1, pl.ds(shard, 1)], tail)
            send_ref[shard] = jnp.concatenate([pooled[: CAP - 8], tail], axis=0).astype(BF)
            send_block(step, which, flip, place, shard, send_ref, recv_ref, send_sem, recv_sem)

    def receive(step):
        flip, _, moves = quad(step)
        wait_for(send_ref.at[pl.ds(0, 4)], recv_sem.at[step])
        arrived, fields, samples = [], [], []
        for move in moves:
            shard = shard_at(flip, move, -1)
            block = recv_ref[shard]
            tail = block[CAP - 16 : CAP].astype(F32)
            arrived.append(block)
            fields.append(tail[14:15])
            samples.append(tail[15:16])
            owners_ref[0, pl.ds(shard, 1)] = fields[-1]
            owners_ref[1, pl.ds(shard, 1)] = samples[-1]
        arrived = jnp.concatenate(arrived, axis=0)
        field = jnp.concatenate(fields, axis=1)
        sample = jnp.concatenate(samples, axis=1)
        in_sample = one_hot(iota((LANES, 4 * LANES), 0).astype(F32) == sample)
        for tile in range(FIELDS):
            member = in_sample * one_hot(field == tile + 1.0)
            sums_ref[tile] += jnp.dot(member, arrived, preferred_element_type=F32)

    paced_exchange(
        send,
        receive,
        [(1, gather[1]), (7, gather[2]), (19, gather[3]), (28, gather[4])],
    )
    wait_for(send_ref.at[pl.ds(0, LANES - 1)], send_sem)
    for tile in range(FIELDS):
        out_ref[:, tile * LANES : (tile + 1) * LANES] = sums_ref[tile].astype(BF)
    gather[5]()


def window_tile(tile):
    start = tile * 4 * SHARD_ROWS
    return min(start // LANES, FIELDS - 2), start


def window_map(tile):
    first, start = window_tile(tile)
    feature = iota((2 * LANES, LANES), 0) + (first * LANES - start)
    place = iota((2 * LANES, LANES), 1)
    row = place % PAD_ROWS
    wanted = (place // PAD_ROWS) * SHARD_ROWS + row
    return jnp.where(row < SHARD_ROWS, one_hot(feature == wanted), jnp.zeros((), BF))


def dense_step(
    feature_ref, label_ref, first_ref, second_ref, third_ref, last_ref,
    grad_ref, packed_ref, padded_ref, network_ref, after_sums,
):
    blocks, padded_rows = first_ref.shape[0], padded_ref.shape[1]
    padded_tiles = padded_rows // LANES
    for tile in range(padded_tiles):
        first, _ = window_tile(tile)
        window = feature_ref[:, first * LANES : (first + 2) * LANES]
        padded = jnp.dot(window, window_map(tile), preferred_element_type=F32)
        padded_ref[:, tile * LANES : (tile + 1) * LANES] = padded.astype(BF)
    first_pre = jnp.concatenate(
        [
            jnp.dot(
                padded_ref[...],
                first_ref[block].reshape(padded_rows, LANES),
                preferred_element_type=F32,
            )
            for block in range(blocks)
        ],
        axis=1,
    )
    first_act, first_slope = act_slope(first_pre)
    first_act = first_act.astype(BF)
    second_act, second_slope = act_slope(
        jnp.dot(first_act, second_ref[...], preferred_element_type=F32)
    )
    second_act = second_act.astype(BF)
    third_act, third_slope = act_slope(
        jnp.dot(second_act, third_ref[...], preferred_element_type=F32)
    )
    third_act = third_act.astype(BF).astype(F32)
    last = last_ref[...].astype(F32)
    last = jnp.concatenate([last[row : row + 1] for row in range(last.shape[0])], axis=1)
    label = jnp.broadcast_to(label_ref[...].astype(F32), (LANES, LANES)).T[:, :1]
    deep = jnp.sum(third_act * last, axis=1, keepdims=True)
    total = jnp.zeros((feature_ref.shape[0], LANES), F32)
    squares = jnp.zeros((feature_ref.shape[0], LANES), F32)
    for tile in range(FIELDS):
        vector = feature_ref[:, tile * LANES : (tile + 1) * LANES].astype(F32)
        total = total + vector
        squares = squares + vector * vector
    pairs = 0.5 * jnp.sum(total * total - squares, axis=1, keepdims=True)
    logit_grad = jax.nn.sigmoid(deep + pairs) - label
    h1, h2 = second_ref.shape
    h3 = third_ref.shape[1]
    start = h1 * h2 // LANES
    end = start + h2 * h3 // LANES
    packed_ref[end:] = jnp.zeros_like(packed_ref[end:])
    grad_out = jnp.sum(logit_grad * third_act, axis=0, keepdims=True)
    for tile in range(h3 // LANES):
        packed_ref[end + 16 * tile : end + 16 * tile + 1] = grad_out[
            :, tile * LANES : (tile + 1) * LANES
        ]
    third_grad = (logit_grad * last * third_slope).astype(BF)
    grad_third = contract(second_act, third_grad, 0, 0)
    for tile in range(h3 // LANES):
        packed_ref[start + tile * h2 : start + (tile + 1) * h2] = grad_third[
            :, tile * LANES : (tile + 1) * LANES
        ]
    second_grad = (contract(third_grad, third_ref[...], 1, 1) * second_slope).astype(BF)
    for tile in range(h2 // LANES):
        packed_ref[tile * h1 : (tile + 1) * h1] = contract(
            first_act, second_grad[:, tile * LANES : (tile + 1) * LANES], 0, 0
        )
    after_sums()
    first_grad = (contract(second_grad, second_ref[...], 1, 1) * first_slope).astype(BF)
    first_grad = first_grad.T
    network_ref[...] = jnp.zeros_like(network_ref)
    parts = []
    for z in range(first_ref.shape[1]):
        weights = [first_ref[block, z].reshape(4 * LANES, LANES) for block in range(blocks)]
        weights = jnp.concatenate(weights, axis=1)
        parts.append(jnp.dot(weights, first_grad, preferred_element_type=F32))
    halves = []
    for part in parts:
        upper = part.astype(BF)
        halves.append((upper, (part - upper.astype(F32)).astype(BF)))
    for tile in range(padded_tiles):
        first, _ = window_tile(tile)
        place = window_map(tile)
        place = jnp.concatenate([place, place], axis=1)
        rows = slice(tile % 4 * LANES, (tile % 4 + 1) * LANES)
        pair = jnp.concatenate([half[rows] for half in halves[tile // 4]], axis=0)
        moved = jnp.dot(place, pair, preferred_element_type=F32)
        network_ref[first] += moved[:LANES]
        network_ref[first + 1] += moved[LANES:]
    for tile in range(FIELDS):
        vector = feature_ref[:, tile * LANES : (tile + 1) * LANES].astype(F32)
        grad_ref[tile * LANES : (tile + 1) * LANES] = (
            network_ref[tile].T + logit_grad * (total - vector)
        ).astype(BF)


def device(**axes):
    emb, dp = lax.axis_index("emb"), lax.axis_index("dp")
    z, y, core = emb // 16, (emb // 2) % 8, emb % 2
    z, y, core = axes.get("z", z), axes.get("y", y), axes.get("core", core)
    return {"emb": z * 16 + y * 2 + core, "dp": axes.get("x", dp)}


def send_to(partner, source, target, send_sem, recv_sem):
    pltpu.make_async_remote_copy(
        source,
        target,
        send_sem,
        recv_sem,
        device_id=partner,
        device_id_type=pl.DeviceIdType.MESH,
    ).start()


def wait_for(block, sem):
    pltpu.make_async_copy(block, block, sem).wait()


def reduce_steps(
    packed_ref, outs, full_ref, from_core, from_x, from_z, from_y, sum_core, sum_x, sum_z,
    send_sem, recv_sem,
):
    emb, x = lax.axis_index("emb"), lax.axis_index("dp")
    z, y, core = emb // 16, (emb // 2) % 8, emb % 2
    other = device(core=1 - core)
    half = packed_ref.shape[0] // 2
    eighth = half // 4

    def over_core():
        theirs = packed_ref.at[pl.ds(pl.multiple_of((1 - core) * half, eighth), half)]
        send_to(other, theirs, from_core, send_sem.at[0], recv_sem.at[0])

    def over_x():
        wait_for(from_core, recv_sem.at[0])
        for part in range(4):
            mine = packed_ref[pl.ds(pl.multiple_of(core * half + part * eighth, eighth), eighth)]
            theirs = from_core[part * eighth : (part + 1) * eighth]
            sum_core[part] = (mine + theirs).reshape(sum_core.shape[1:]).astype(BF)
        for step in range(1, 4):
            to = (x + step) % 4
            send_to(device(x=to), sum_core.at[to], from_x.at[x], send_sem.at[1], recv_sem.at[1])
        from_x[x] = sum_core[x]

    def over_z():
        wait_for(from_x.at[pl.ds(0, 3)], recv_sem.at[1])
        for part in range(8):
            terms = [from_x[one, part].astype(F32) for one in range(4)]
            sum_x[part] = ((terms[0] + terms[1]) + (terms[2] + terms[3])).astype(BF)
        for step in range(1, 8):
            to = (z + step) % 8
            send_to(device(z=to), sum_x.at[to], from_z.at[z], send_sem.at[2], recv_sem.at[2])
        from_z[z] = sum_x[z]

    def over_y():
        wait_for(from_z.at[pl.ds(0, 7)], recv_sem.at[2])
        sum_z[...] = jnp.sum(from_z[...].astype(F32), axis=0).astype(BF)
        for step in range(1, 8):
            to = (y + step) % 8
            send_to(device(y=to), sum_z, from_y.at[y], send_sem.at[3], recv_sem.at[3])
        from_y[y] = sum_z[...]

    def gather_z():
        wait_for(from_y.at[pl.ds(0, 7)], recv_sem.at[3])
        full_ref[core, x, z] = jnp.sum(from_y[...].astype(F32), axis=0).astype(BF)
        mine = full_ref.at[core, x, z]
        for step in range(1, 8):
            send_to(device(z=(z + step) % 8), mine, mine, send_sem.at[4], recv_sem.at[4])

    def gather_x():
        wait_for(full_ref.at[core, x, pl.ds(0, 7)], recv_sem.at[4])
        mine = full_ref.at[core, x]
        for step in range(1, 4):
            send_to(device(x=(x + step) % 4), mine, mine, send_sem.at[5], recv_sem.at[5])

    def gather_core():
        wait_for(full_ref.at[core, pl.ds(0, 3)], recv_sem.at[5])
        mine = full_ref.at[core]
        send_to(other, mine, mine, send_sem.at[6], recv_sem.at[6])

    def finish():
        wait_for(full_ref.at[0], recv_sem.at[6])
        wait_for(from_core, send_sem.at[0])
        wait_for(from_x.at[pl.ds(0, 3)], send_sem.at[1])
        wait_for(from_z.at[pl.ds(0, 7)], send_sem.at[2])
        wait_for(from_y.at[pl.ds(0, 7)], send_sem.at[3])
        wait_for(full_ref.at[core, x, pl.ds(0, 7)], send_sem.at[4])
        wait_for(full_ref.at[core, pl.ds(0, 3)], send_sem.at[5])
        wait_for(full_ref.at[0], send_sem.at[6])
        for place, ref, column, row in grad_places(*outs):
            half, place = divmod(place, 4 * 8 * GRAD_ROWS)
            quarter, place = divmod(place, 8 * GRAD_ROWS)
            part, inside = divmod(place, GRAD_ROWS)
            block = full_ref[half, quarter, part, inside : inside + 16]
            ref[row : row + 16, column : column + LANES] = block.astype(F32)

    return [over_core, over_x, over_z, over_y, gather_z, gather_x, gather_core, finish]


GRAD_ROWS = 96


def grad_places(second_ref, third_ref, out_ref):
    place = 0
    for ref in (second_ref, third_ref, out_ref):
        for column in range(0, ref.shape[1], LANES):
            for row in range(0, ref.shape[0], 16):
                yield place, ref, column, row
                place += 16


def backward_exchange(
    numbers_ref, owners_ref, grad_ref, out_ref, send_ref, recv_ref, send_sem, recv_sem, reduce
):
    def send(step):
        flip, place, moves = quad(step)
        partners = [shard_at(flip, move, 1) for move in moves]
        members = []
        for shard in partners:
            square = (LANES, LANES)
            field = jnp.broadcast_to(owners_ref[0, pl.ds(shard, 1)], square).T[:CAP].astype(BF)
            sample = jnp.broadcast_to(owners_ref[1, pl.ds(shard, 1)], square).T[:CAP]
            in_sample = one_hot(iota((CAP, LANES), 1).astype(F32) == sample)
            none = jnp.zeros_like(in_sample)
            members.append(
                jnp.concatenate(
                    [
                        jnp.where(field == jnp.array(tile + 1.0, BF), in_sample, none)
                        for tile in range(FIELDS)
                    ],
                    axis=1,
                )
            )
        members = jnp.concatenate(members, axis=0)
        spread = jnp.dot(members, grad_ref[...], preferred_element_type=F32).astype(BF)
        for which, shard in enumerate(partners):
            send_ref[shard] = spread[which * CAP : (which + 1) * CAP]
            send_block(step, which, flip, place, shard, send_ref, recv_ref, send_sem, recv_sem)

    def receive(step):
        flip, _, moves = quad(step)
        wait_for(send_ref.at[pl.ds(0, 4)], recv_sem.at[step])
        partners = [shard_at(flip, move, -1) for move in moves]
        arrived = jnp.concatenate([recv_ref[shard] for shard in partners], axis=0)
        high, low = number_rows(numbers_ref, partners)
        counts = count_rows(high, low, out_ref.shape[0] // LANES)
        out_ref[...] += jnp.dot(counts, arrived, preferred_element_type=F32)

    paced_exchange(
        send,
        receive,
        [
            (2, reduce[1]),
            (9, reduce[2]),
            (14, reduce[3]),
            (19, reduce[4]),
            (24, reduce[5]),
            (32, reduce[6]),
        ],
    )
    reduce[7]()
    wait_for(send_ref.at[pl.ds(0, LANES - 1)], send_sem)


def remote_params(collective_id):
    return pltpu.CompilerParams(
        vmem_limit_bytes=46 << 20, collective_id=collective_id, has_side_effects=True
    )


WHOLE = pl.BlockSpec(memory_space=pltpu.VMEM)


def cost(flops, bytes_accessed):
    return pl.CostEstimate(flops=flops, bytes_accessed=bytes_accessed, transcendentals=0)


def per_device(
    table_rows,
    piece_ids,
    piece_counts,
    piece_dest,
    piece_target,
    labels,
    w_first,
    w_second,
    w_third,
    w_out,
):
    shards = lax.axis_size("emb")
    pieces = piece_ids.shape[0]
    touched, width = table_rows.shape
    samples = labels.shape[0]
    h1, h2 = w_second.shape
    h3 = w_third.shape[1]

    blocks = h1 // LANES
    padded = shards * PAD_ROWS
    shard = jnp.pad(w_first, ((0, PAD_ROWS - SHARD_ROWS), (0, 0)))
    shard = shard.reshape(PAD_ROWS, blocks, LANES).transpose(1, 0, 2)
    part = (GRAD_ROWS, LANES)
    row_grad, grad_second, grad_third, grad_out = pl.pallas_call(
        step_kernel,
        out_shape=(
            jax.ShapeDtypeStruct((touched, width), F32),
            jax.ShapeDtypeStruct((h1, h2), F32),
            jax.ShapeDtypeStruct((h2, h3), F32),
            jax.ShapeDtypeStruct((16, h3), F32),
        ),
        in_specs=[WHOLE] * 10,
        out_specs=(WHOLE,) * 4,
        scratch_shapes=[
            pltpu.VMEM((10, shards, LANES), F32),
            pltpu.VMEM((2, shards, LANES), F32),
            pltpu.VMEM((blocks, 8, 8, 2, PAD_ROWS, LANES), BF),
            pltpu.VMEM((samples, FIELDS * width), BF),
            pltpu.VMEM((FIELDS * samples, width), BF),
            pltpu.VMEM((64 * GRAD_ROWS, LANES), F32),
            pltpu.VMEM((samples, padded), BF),
            pltpu.VMEM((FIELDS, samples, width), F32),
            pltpu.VMEM((shards, CAP, width), BF),
            pltpu.VMEM((shards, LANES, width), BF),
            pltpu.VMEM((shards, LANES, width), BF),
            pltpu.SemaphoreType.DMA,
            pltpu.SemaphoreType.DMA((STEPS,)),
            pltpu.SemaphoreType.DMA,
            pltpu.SemaphoreType.DMA((STEPS,)),
            pltpu.SemaphoreType.DMA((6,)),
            pltpu.SemaphoreType.DMA((9,)),
            pltpu.VMEM((2, 4, 8) + part, BF),
            pltpu.VMEM((32 * GRAD_ROWS, LANES), F32),
            pltpu.VMEM((4, 8) + part, BF),
            pltpu.VMEM((8,) + part, BF),
            pltpu.VMEM((8,) + part, BF),
            pltpu.VMEM((4, 8) + part, BF),
            pltpu.VMEM((8,) + part, BF),
            pltpu.VMEM(part, BF),
            pltpu.SemaphoreType.DMA((7,)),
            pltpu.SemaphoreType.DMA((7,)),
        ],
        compiler_params=remote_params(0),
        cost_estimate=cost(4 * shards * CAP * FIELDS * samples * width, 400_000_000),
    )(
        piece_dest.reshape(1, pieces),
        piece_target.reshape(pieces // LANES, LANES),
        piece_counts.reshape(pieces // LANES, LANES),
        piece_ids.T,
        table_rows,
        shard,
        labels.reshape(1, samples),
        w_second,
        w_third,
        w_out.reshape(h3 // LANES, LANES),
    )
    return (row_grad, grad_second, grad_third, grad_out[0])


def solution(mesh):
    in_specs = (
        P(("emb", "dp"), None),
        P(("emb", "dp"), None),
        P(("emb", "dp")),
        P(("emb", "dp"), None),
        P(("emb", "dp")),
        P(("emb", "dp")),
        P("emb", None),
        P(),
        P(),
        P(),
    )
    out_specs = (P(("emb", "dp"), None), P(), P(), P())
    return jax.shard_map(
        per_device, mesh=mesh, in_specs=in_specs, out_specs=out_specs, check_vma=False
    )
```
